128 devices in a mesh: dp: 8 (over x, core), shard: 2 (over z_lo), ctx: 8 (over z_hi, y).
Axes of the slice: x: 4, y: 4, z: 4 (z_hi: 2, z_lo: 2; z = z_hi * 2 + z_lo), core: 2. Of those that a mesh axis runs over, the one named last changes fastest.
Arguments:
- inputs: bfloat16 [16384, 4096], P(('dp', 'shard', 'ctx')), may hold values from -24 to 24
- queries: bfloat16 [16384, 4096], P(('dp', 'shard', 'ctx')), may hold values from -272 to 272
- out_grad: bfloat16 [16384, 4096], P(('dp', 'shard', 'ctx')), may hold values from -6 to 6
- span_ids: int32 [8, 16, 2], P('dp'), may hold values from 0 to 31, as said below
- norm_gain: bfloat16 [4096], P(('shard', 'ctx')), may hold values from 0.5 to 1.5
- key_weight: bfloat16 [4096, 512], P(('shard', 'ctx')), may hold values from -0.09375 to 0.09375
- value_weight: bfloat16 [4096, 512], P(('shard', 'ctx')), may hold values from -0.09375 to 0.09375
Outputs:
- attention_out: bfloat16 [16384, 4096], P(('dp', 'shard', 'ctx'))
- query_grad: bfloat16 [16384, 4096], P(('dp', 'shard', 'ctx'))
- input_grad: bfloat16 [16384, 4096], P(('dp', 'shard', 'ctx'))
- key_weight_grad: float32 [4096, 512], P(('shard', 'ctx'))
- value_weight_grad: float32 [4096, 512], P(('shard', 'ctx'))
- gain_grad: float32 [4096], P(('shard', 'ctx'))
The draws below stay inside these ranges and needn't reach their ends.
Inputs may be any that keep to these rules, and one draw needn't show every extreme that they name: `span_ids`: in each replica the 16 rows together hold every span number once; a row holds some c and 31 - c, in either order.
All inputs are finite; a program needn't handle non-finite values.
Results may differ from the reference program's by a relative error of at most 0.012.
The reference program's roundings to bfloat16 on the way (of `normed`, `keys`, `values`, `weights_low`, `score_grad`, `probs_low`, `key_grad` and `value_grad`) count: a program that leaves them out, or rounds other values in their place, can miss the bound.
Values may be sent and summed in bfloat16 or wider, within the bound.
A program may use at most 128 MiB of HBM per device.

```python
import math
from functools import partial
import jax
import jax.numpy as jnp
from jax import lax

D = 4096
KV_HEADS = 4
HEAD_DIM = 128
SPAN = 64
GROUP = 8
Q_WIDTH = 4096
KV_WIDTH = 512
RANKS = 16
REPLICAS = 8
SEQ = 2048
TOKENS = 16384


def draw_queries(key, part):
    key = jax.random.fold_in(key, 17)
    base_key = jax.random.fold_in(key, 0)
    return jnp.clip(jax.random.normal(base_key, (TOKENS, Q_WIDTH), jnp.float32), -6.0, 6.0).astype(jnp.bfloat16)


def draw_out_grad(key, part):
    key = jax.random.fold_in(key, 23)
    base = jnp.clip(jax.random.normal(key, (TOKENS, Q_WIDTH), jnp.float32), -6.0, 6.0)
    return base.astype(jnp.bfloat16)


def draw_span_ids(key, part):
    key = jax.random.fold_in(key, 5)
    replica_keys = jax.random.split(key, REPLICAS)

    def one_replica(replica_key):
        order_key, flip_key = jax.random.split(replica_key)
        lower = jax.random.permutation(order_key, RANKS).astype(jnp.int32)
        upper = 2 * RANKS - 1 - lower
        flips = jax.random.randint(flip_key, (RANKS,), 0, 2)
        first = jnp.where(flips == 1, upper, lower)
        second = jnp.where(flips == 1, lower, upper)
        return jnp.stack([first, second], axis=1).astype(jnp.int32)
    return jax.vmap(one_replica)(replica_keys)


def strengthened(entries, stream_key, source, target, blocks, factor):
    owner, partner = [(jnp.arange(entries.shape[dim]) // (entries.shape[dim] // blocks)).reshape([-1 if axis == dim else 1 for axis in range(entries.ndim)]) for dim in (source, target)]
    chosen = jax.random.permutation(stream_key, blocks)[partner]
    strong = (owner == chosen) | (owner == (partner + blocks // 2) % blocks)
    return jnp.where(strong, factor * entries, entries)


def block_scale(own_key, shape, pieces, low, top_value):
    def one(dim, parts):
        steps = jax.random.uniform(jax.random.fold_in(jax.random.fold_in(own_key, 6), dim), (parts,), jnp.float32, low / len(pieces), top_value / len(pieces))
        return jnp.repeat(jnp.exp(steps), shape[dim] // parts).reshape((-1,) + (1,) * (len(shape) - dim - 1))

    loudness = one(*pieces[0])
    for cut in pieces[1:]:
        loudness = loudness * one(*cut)
    return loudness


def bell_draw(stream_key, shape, width, most, shards=(), kind=jnp.bfloat16):
    gain = block_scale(stream_key, shape, shards, -0.22, 0.18) if shards else 1.0
    entries = jax.random.normal(stream_key, shape, jnp.float32) * width * gain
    return jnp.minimum(jnp.maximum(entries, -most), most).astype(kind)


def gaussian_with(own_key, dims, spread, limit, cuts, heavy, kind=jnp.bfloat16):
    values = spread * jax.random.normal(own_key, dims, jnp.float32)
    if cuts:
        values = values * block_scale(own_key, dims, cuts, -0.22, 0.18)
    return jnp.clip(strengthened(values, jax.random.fold_in(own_key, 3), *heavy), -limit, limit).astype(kind)


def setup_inputs(seed: int = 0) -> dict:
    streams_of = jax.random.split(jax.random.key(seed), 8)
    return {
        "inputs": gaussian_with(streams_of[0], (TOKENS, D), 1.0, 24.0, ((0, 128),), (0, 1, 128, 5.5)),
        "queries": draw_queries(jax.random.fold_in(streams_of[7], 71), 0),
        "out_grad": draw_out_grad(jax.random.fold_in(streams_of[7], 71), 0),
        "span_ids": draw_span_ids(jax.random.fold_in(streams_of[7], 71), 0),
        "norm_gain": jnp.clip(1.0 + 0.1 * jax.random.normal(streams_of[4], (D,), jnp.float32), 0.5, 1.5).astype(jnp.bfloat16),
        "key_weight": bell_draw(streams_of[5], (D, KV_WIDTH), D ** -0.5, 0.09375, ((0, 16),)),
        "value_weight": bell_draw(streams_of[6], (D, KV_WIDTH), D ** -0.5, 0.09375, ((0, 16),)),
    }


EPSILON = 1e-05
ROPE_BASE = 500000.0

def rope_tables(positions, head_size):
    half = head_size // 2
    frequency = jnp.exp(-math.log(ROPE_BASE) * (2.0 * jnp.arange(half, dtype=jnp.float32) / head_size))
    angles = positions.astype(jnp.float32)[:, None] * frequency[None, :]
    return (jnp.cos(angles)[:, None, :], jnp.sin(angles)[:, None, :])

def rotate(vectors, cosine, sine, direction):
    half = vectors.shape[-1] // 2
    first = vectors[..., :half]
    second = vectors[..., half:]
    return jnp.concatenate([first * cosine - direction * second * sine, second * cosine + direction * first * sine], axis=-1)

def replica_positions(owner_ids):
    flat_ids = owner_ids.reshape(-1)
    row_index = jnp.arange(SEQ, dtype=jnp.int32)
    return flat_ids[row_index // SPAN] * SPAN + row_index % SPAN

def head_group(operands, positions):
    grouped_q, key_head, value_head, grouped_g = operands
    scale = HEAD_DIM ** (-0.5)
    query_f = grouped_q.astype(jnp.float32)
    key_f = key_head.astype(jnp.float32)
    value_f = value_head.astype(jnp.float32)
    grad_f = grouped_g.astype(jnp.float32)
    visible = positions[None, :] <= positions[:, None]
    scores = jnp.einsum('gtd,nd->gtn', query_f, key_f) * scale
    row_max = lax.optimization_barrier(jnp.max(jnp.where(visible, scores, -1e+30), axis=-1))
    weights = jnp.where(visible, jnp.exp(scores - row_max[..., None]), 0.0)
    totals = lax.optimization_barrier(jnp.sum(weights, axis=-1))
    weights_low = lax.optimization_barrier(weights.astype(jnp.bfloat16)).astype(jnp.float32)
    attended = (jnp.einsum('gtn,nd->gtd', weights_low, value_f) / totals[..., None]).astype(jnp.bfloat16)
    attended_f = lax.optimization_barrier(attended).astype(jnp.float32)
    log_total = row_max + jnp.log(totals)
    probs = jnp.where(visible, jnp.exp(scores - log_total[..., None]), 0.0)
    value_dots = jnp.einsum('gtd,nd->gtn', grad_f, value_f)
    row_dots = lax.optimization_barrier(jnp.sum(grad_f * attended_f, axis=-1))
    score_grad = (probs * (value_dots - row_dots[..., None]) * scale).astype(jnp.bfloat16)
    score_grad = lax.optimization_barrier(score_grad).astype(jnp.float32)
    probs_low = lax.optimization_barrier(probs.astype(jnp.bfloat16)).astype(jnp.float32)
    query_grad = jnp.einsum('gtn,nd->gtd', score_grad, key_f).astype(jnp.bfloat16)
    key_grad = jnp.einsum('gtn,gtd->nd', score_grad, query_f)
    value_grad = jnp.einsum('gtn,gtd->nd', probs_low, grad_f)
    return (attended, query_grad, key_grad, value_grad)

def one_replica(operands, norm_gain, key_weight, value_weight):
    inputs, queries, out_grad, owner_ids = operands
    positions = replica_positions(owner_ids)
    input_f = inputs.astype(jnp.float32)
    inverse_rms = lax.rsqrt(lax.optimization_barrier(jnp.mean(input_f * input_f, axis=-1, keepdims=True)) + EPSILON)
    unit_rows = input_f * inverse_rms
    gain_f = norm_gain.astype(jnp.float32)
    normed = (unit_rows * gain_f).astype(jnp.bfloat16)
    key_raw = jnp.dot(normed, key_weight, preferred_element_type=jnp.float32)
    value_raw = jnp.dot(normed, value_weight, preferred_element_type=jnp.float32)
    cosine, sine = rope_tables(positions, HEAD_DIM)
    keys = rotate(key_raw.reshape(SEQ, KV_HEADS, HEAD_DIM), cosine, sine, 1.0).astype(jnp.bfloat16)
    values = value_raw.astype(jnp.bfloat16).reshape(SEQ, KV_HEADS, HEAD_DIM)
    grouped_q = queries.reshape(SEQ, KV_HEADS, GROUP, HEAD_DIM).transpose(1, 2, 0, 3)
    grouped_g = out_grad.reshape(SEQ, KV_HEADS, GROUP, HEAD_DIM).transpose(1, 2, 0, 3)
    attended, query_grad, key_rot, value_sum = lax.map(partial(head_group, positions=positions), (grouped_q, keys.transpose(1, 0, 2), values.transpose(1, 0, 2), grouped_g))
    attended = attended.transpose(2, 0, 1, 3).reshape(SEQ, Q_WIDTH)
    query_grad = query_grad.transpose(2, 0, 1, 3).reshape(SEQ, Q_WIDTH)
    key_grad = rotate(key_rot.transpose(1, 0, 2), cosine, sine, -1.0).reshape(SEQ, KV_WIDTH).astype(jnp.bfloat16)
    value_grad = value_sum.transpose(1, 0, 2).reshape(SEQ, KV_WIDTH).astype(jnp.bfloat16)
    normed_grad = jnp.dot(key_grad, key_weight.T, preferred_element_type=jnp.float32) + jnp.dot(value_grad, value_weight.T, preferred_element_type=jnp.float32)
    unit_grad = normed_grad * gain_f
    input_grad = (inverse_rms * (unit_grad - unit_rows * lax.optimization_barrier(jnp.mean(unit_grad * unit_rows, axis=-1, keepdims=True)))).astype(jnp.bfloat16)
    key_term = jnp.dot(normed.T, key_grad, preferred_element_type=jnp.float32)
    value_term = jnp.dot(normed.T, value_grad, preferred_element_type=jnp.float32)
    gain_term = lax.optimization_barrier(jnp.sum(unit_rows * normed_grad, axis=0))
    return (attended, query_grad, input_grad, key_term, value_term, gain_term)

def reference(inputs, queries, out_grad, span_ids, norm_gain, key_weight, value_weight):
    stacked = (inputs.reshape(REPLICAS, SEQ, D), queries.reshape(REPLICAS, SEQ, Q_WIDTH), out_grad.reshape(REPLICAS, SEQ, Q_WIDTH), span_ids)
    attended, query_grad, input_grad, key_term, value_term, gain_term = lax.map(partial(one_replica, norm_gain=norm_gain, key_weight=key_weight, value_weight=value_weight), stacked)
    return (attended.reshape(TOKENS, Q_WIDTH), query_grad.reshape(TOKENS, Q_WIDTH), input_grad.reshape(TOKENS, D), lax.optimization_barrier(jnp.sum(key_term, axis=0)), lax.optimization_barrier(jnp.sum(value_term, axis=0)), lax.optimization_barrier(jnp.sum(gain_term, axis=0)))
```

```python
import functools
import math

import jax
import jax.numpy as jnp
from jax import lax
from jax.experimental import pallas as pl
from jax.experimental.pallas import tpu as pltpu
from jax.sharding import PartitionSpec as P

HEAD = 128
HEADS = 4
GROUP = 8
SPAN = 64
RANKS = 16
ROWS = 128
FEATURES = 4096
SHARE = 256
WIDTH = 512
BLOCK = 272
EPSILON = 1e-05
ROPE_BASE = 500000.0
NEG_FILL = -1e30
SCALE = HEAD ** (-0.5)
EXP_SCALE = SCALE * math.log2(math.e)
MESH = pl.DeviceIdType.MESH
F32 = jnp.float32
BF16 = jnp.bfloat16
NT = (((1,), (1,)), ((), ()))


def device_at(x, core, y, z):
    return (x * 2 + core, z % 2, (z // 2) * 4 + y)


def rank_at(y, z):
    return (z % 2) * 8 + (z // 2) * 4 + y


def dot(a, b):
    return jnp.dot(a, b, preferred_element_type=F32)


def dot_nt(a, b):
    return lax.dot_general(a, b, NT, preferred_element_type=F32)


class Place:
    def __init__(self):
        dp = lax.axis_index("dp")
        shard = lax.axis_index("shard")
        ctx = lax.axis_index("ctx")
        self.x = dp // 2
        self.core = dp % 2
        self.y = ctx % 4
        self.z = (ctx // 4) * 2 + shard
        self.rank = rank_at(self.y, self.z)

    def partner(self):
        return device_at(self.x, 1 - self.core, self.y, self.z)

    def along_x(self, step):
        return device_at((self.x + step) % 4, self.core, self.y, self.z)


class Route:
    def __init__(self, place, first, send, recv):
        self.place, self.first, self.send_sems, self.recv_sems = place, first, send, recv

    def point(self, da, db):
        dy, dz = (da, db) if self.first == "y" else (db, da)
        return (self.place.y + dy + 4) % 4, (self.place.z + dz + 4) % 4

    def rank(self, da, db):
        return rank_at(*self.point(da, db))

    def device(self, da, db):
        return device_at(self.place.x, self.place.core, *self.point(da, db))

    def copy(self, index, src, dst, to):
        return pltpu.make_async_remote_copy(
            src_ref=src,
            dst_ref=dst,
            send_sem=self.send_sems.at[index],
            recv_sem=self.recv_sems.at[index],
            device_id=self.device(*to),
            device_id_type=MESH,
        )


def gather_table():
    table = [
        ((0, 0), "full", (1, 0), (-1, 0)),
        ((0, 0), "full", (-1, 0), (1, 0)),
        ((-1, 0), "lo", (1, 0), (2, 0)),
        ((1, 0), "hi", (-1, 0), (2, 0)),
    ]
    for da in (0, -1, 1, 2):
        table += [
            ((da, 0), "full", (0, 1), (da, -1)),
            ((da, 0), "full", (0, -1), (da, 1)),
            ((da, -1), "lo", (0, 1), (da, 2)),
            ((da, 1), "hi", (0, -1), (da, 2)),
        ]
    return table


class Gather(Route):
    table = gather_table()
    plan = (
        ("s0", "s1", "s4", "s5"),
        ("r0", "s2", "s8", "s9", "r1", "s3", "s12", "s13", "r4", "s6", "r5", "s7"),
        ("r2", "r3", "s16", "s17", "r8", "s10", "r9", "s11", "r12", "s14", "r13", "s15", "r6", "r7"),
        ("r16", "s18", "r17", "s19", "r10", "r11", "r14", "r15"),
        ("r18", "r19"),
    )
    whole = {0: 0, 1: 1, 3: 2, 4: 4, 5: 5, 7: 6}

    def __init__(self, place, first, slot, send, recv):
        super().__init__(place, first, send, recv)
        self.slot = slot

    def send(self, m):
        block, part, to, _ = self.table[m]
        ref = self.slot(self.rank(*block), part)
        return self.copy(m, ref, ref, to)

    def arrival(self, m):
        _, part, to, block = self.table[m]
        ref = self.slot(self.rank(*block), part)
        return self.copy(m, ref, ref, to)

    def stage(self, number, arrived=None):
        for item in self.plan[number]:
            m = int(item[1:])
            if item[0] == "s":
                self.send(m).start()
                continue
            self.arrival(m).wait_recv()
            if arrived is not None:
                _, part, _, block = self.table[m]
                if part == "full" or m in (3, 7, 11, 15, 19):
                    arrived(block)

    def drain(self):
        for m in range(20):
            self.send(m).wait_send()


class Scatter(Route):
    order = (2, 1, -1, 0)

    def __init__(self, place, first, slot, halves, wholes, send, recv):
        super().__init__(place, first, send, recv)
        self.slot, self.halves, self.wholes = slot, halves, wholes

    def message(self, m):
        if m < 16:
            i, k = m // 4, m % 4
            da = self.order[i]
            blocks = ((da, 2), (da, 2), (da, 1), (da, -1))
            to = ((0, 1), (0, -1))[k % 2]
        else:
            i, k = 4, m - 16
            blocks = ((2, 0), (2, 0), (1, 0), (-1, 0))
            to = ((1, 0), (-1, 0))[k % 2]
        part = ("lo", "hi", "full", "full")[k]
        src = self.slot(self.rank(*blocks[k]), part)
        dst = self.halves(i, part) if k < 2 else self.wholes(i, k - 2)
        return self.copy(m, src, dst, to)

    def start(self, m):
        self.message(m).start()

    def arrive(self, m):
        self.message(m).wait_recv()

    def add(self, block, part, *refs):
        ref = self.slot(self.rank(*block), part)
        total = ref[...].astype(F32)
        for other in refs:
            total = total + other[...].astype(F32)
        ref[...] = total.astype(BF16)

    def stage(self, number):
        if number == 0:
            for i in range(4):
                self.start(4 * i)
                self.start(4 * i + 1)
        elif number == 1:
            for i, da in enumerate(self.order):
                self.arrive(4 * i)
                self.add((da, 1), "lo", self.halves(i, "lo"))
                self.start(4 * i + 2)
                self.arrive(4 * i + 1)
                self.add((da, -1), "hi", self.halves(i, "hi"))
                self.start(4 * i + 3)
        elif number == 2:
            for i, da in enumerate(self.order):
                self.arrive(4 * i + 2)
                self.arrive(4 * i + 3)
                self.add((da, 0), "full", self.wholes(i, 0), self.wholes(i, 1))
                if i == 0:
                    self.start(16)
                    self.start(17)
        elif number == 3:
            self.arrive(16)
            self.add((1, 0), "lo", self.halves(4, "lo"))
            self.start(18)
            self.arrive(17)
            self.add((-1, 0), "hi", self.halves(4, "hi"))
            self.start(19)
        else:
            self.arrive(18)
            self.arrive(19)

    def total(self):
        own = self.slot(self.rank(0, 0), "full")[...].astype(F32)
        return own + self.wholes(4, 0)[...].astype(F32) + self.wholes(4, 1)[...].astype(F32)

    def drain(self):
        for m in range(20):
            self.message(m).wait_send()


def weight_rows(kind, part):
    if kind == 0:
        return {"full": pl.ds(0, 128), "lo": pl.ds(0, 64), "hi": pl.ds(64, 64)}[part]
    return {"full": pl.ds(128, 144), "lo": pl.ds(128, 64), "hi": pl.ds(192, 80)}[part]


def kernel(
    x_ref, q_ref, g_ref, spans_ref, kpos_ref, gain_ref, wk_ref, wv_ref, cos_ref, sin_ref,
    out_ref, dq_ref, dx_ref, dwk_ref, dwv_ref, dgain_ref,
    wbuf, kvbuf, qs, gs, qt, gt, probs, dscore, grads, kv_half, kv_whole, dkv, ngrad,
    terms, pair, w_half, w_whole, x_send, x_recv, x_gain, final, inv_ref,
    w_send, w_recv, hand_send, hand_recv, kv_send, kv_recv, rs_send, rs_recv,
    pair_send, pair_recv, ws_send, ws_recv, x_ssem, x_rsem,
):
    me = Place()
    barrier = pltpu.get_barrier_semaphore()
    others = [device_at(me.x, me.core, (me.y + d) % 4, me.z) for d in (1, 3)]
    others += [device_at(me.x, me.core, me.y, (me.z + d) % 4) for d in (1, 3)]
    others += [me.along_x(d) for d in (1, 2, 3)] + [me.partner()]
    for other in others:
        pl.semaphore_signal(barrier, inc=1, device_id=other, device_id_type=MESH)

    for kind, ref in ((0, wk_ref), (1, wv_ref)):
        wbuf[kind, me.rank, 0:SHARE, :] = ref[...]
        wbuf[kind, me.rank, SHARE:BLOCK, 0:SHARE] = jnp.broadcast_to(gain_ref[...], (16, SHARE))
        wbuf[kind, me.rank, SHARE:BLOCK, SHARE:WIDTH] = jnp.zeros((16, WIDTH - SHARE), BF16)
    pl.semaphore_wait(barrier, len(others))

    def hand(kind, route, block):
        index = 4 * ((block[0] + 4) % 4) + (block[1] + 4) % 4
        return pltpu.make_async_remote_copy(
            src_ref=wbuf.at[me.core, route.rank(*block), weight_rows(kind, "full")],
            dst_ref=wbuf.at[me.core, route.rank(*block), weight_rows(kind, "full")],
            send_sem=hand_send.at[kind, index],
            recv_sem=hand_recv.at[kind, index],
            device_id=me.partner(),
            device_id_type=MESH,
        )

    def handed(kind, route, block):
        index = 4 * ((block[0] + 4) % 4) + (block[1] + 4) % 4
        return pltpu.make_async_remote_copy(
            src_ref=wbuf.at[1 - me.core, route.rank(*block), weight_rows(kind, "full")],
            dst_ref=wbuf.at[1 - me.core, route.rank(*block), weight_rows(kind, "full")],
            send_sem=hand_send.at[kind, index],
            recv_sem=hand_recv.at[kind, index],
            device_id=me.partner(),
            device_id_type=MESH,
        )

    w_routes = [
        Gather(
            me,
            "yz"[kind],
            lambda rank, part, kind=kind: wbuf.at[me.core, rank, weight_rows(kind, part)],
            w_send.at[kind],
            w_recv.at[kind],
        )
        for kind in range(2)
    ]
    for route in w_routes:
        route.stage(0)

    squares = jnp.zeros((ROWS, HEAD), F32)
    for c in range(FEATURES // HEAD):
        piece = x_ref[:, c * HEAD : (c + 1) * HEAD].astype(F32)
        squares = squares + piece * piece
    inv_ref[...] = lax.rsqrt(
        jnp.sum(squares, axis=-1, keepdims=True) * (1.0 / FEATURES) + EPSILON
    )
    for number in range(1, 5):
        for kind, route in enumerate(w_routes):
            route.stage(
                number, lambda block, kind=kind, route=route: hand(kind, route, block).start()
            )
    blocks = [(a, b) for a in (0, -1, 1, 2) for b in (0, -1, 1, 2) if (a, b) != (0, 0)]
    for kind, route in enumerate(w_routes):
        for block in blocks:
            handed(kind, route, block).wait_recv()

    inverse = inv_ref[...]

    def unit_piece(r):
        return x_ref[:, pl.ds(pl.multiple_of(r * SHARE, SHARE), SHARE)].astype(F32) * inverse

    def gain_piece(r):
        return wbuf[0, r, SHARE:BLOCK, 0:SHARE].astype(F32)[0:1, :]

    def project(r, state):
        normed = (unit_piece(r) * gain_piece(r)).astype(BF16)
        return (
            state[0] + dot(normed, wbuf[0, r, 0:SHARE, :]),
            state[1] + dot(normed, wbuf[1, r, 0:SHARE, :]),
        )

    zero = jnp.zeros((ROWS, WIDTH), F32)
    key_raw, value_raw = lax.fori_loop(0, RANKS, project, (zero, zero))
    first_span = spans_ref[2 * me.rank]
    second_span = spans_ref[2 * me.rank + 1]
    flip = first_span > second_span
    low_span = jnp.minimum(first_span, second_span)
    high_span = jnp.maximum(first_span, second_span)
    cosine, sine = cos_ref[...], sin_ref[...]
    for h in range(HEADS):
        part = key_raw[:, h * HEAD : (h + 1) * HEAD]
        key = part * cosine + pltpu.roll(part, HEAD // 2, 1) * sine
        for kind, array in ((0, key), (1, value_raw[:, h * HEAD : (h + 1) * HEAD])):
            kvbuf[kind, me.rank, 0, h] = jnp.where(flip, array[SPAN:], array[:SPAN]).astype(BF16)
            kvbuf[kind, me.rank, 1, h] = jnp.where(flip, array[:SPAN], array[SPAN:]).astype(BF16)

    def kv_slot(kind, rank, part):
        ref = kvbuf.at[kind, rank]
        return {"full": ref, "lo": ref.at[0], "hi": ref.at[1]}[part]

    kv_routes = [
        Gather(
            me,
            "yz"[kind],
            lambda rank, part, kind=kind: kv_slot(kind, rank, part),
            kv_send.at[kind],
            kv_recv.at[kind],
        )
        for kind in range(2)
    ]
    for number in range(5):
        for route in kv_routes:
            route.stage(number)

    token = lax.broadcasted_iota(jnp.int32, (ROWS, 1), 0) % SPAN
    q_pos = (low_span * SPAN + token, high_span * SPAN + token)

    def scatters(h):
        def slot(kind, rank, part):
            ref = grads.at[h, kind, rank]
            return {"full": ref, "lo": ref.at[0], "hi": ref.at[1]}[part]

        return [
            Scatter(
                me,
                "yz"[kind],
                lambda rank, part, kind=kind: slot(kind, rank, part),
                lambda i, part, kind=kind: kv_half.at[h, kind, i, 0 if part == "lo" else 1],
                lambda i, side, kind=kind: kv_whole.at[h, kind, i, side],
                rs_send.at[h, kind],
                rs_recv.at[h, kind],
            )
            for kind in range(2)
        ]

    def serve(h, number):
        @pl.when(h >= 0)
        def _():
            routes = scatters(jnp.maximum(h, 0))
            for route in routes:
                route.stage(number)
            if number < 4:
                return
            for kind, route in enumerate(routes):
                total = route.total()
                low, high = total[0], total[1]
                total = jnp.concatenate(
                    [jnp.where(flip, high, low), jnp.where(flip, low, high)], axis=0
                )
                if kind == 0:
                    total = total * cos_ref[...] - pltpu.roll(total, HEAD // 2, 1) * sin_ref[...]
                else:
                    total = total * (1.0 / SCALE)
                column = pl.multiple_of(kind * WIDTH + jnp.maximum(h, 0) * HEAD, HEAD)
                dkv[:, pl.ds(column, HEAD)] = total.astype(BF16)

    def one_head(h, carry):
        for n in range(GROUP):
            column = pl.ds(pl.multiple_of((h * GROUP + n) * HEAD, HEAD), HEAD)
            for source, target in ((q_ref, qs), (g_ref, gs)):
                first, second = source[0:SPAN, column], source[SPAN:ROWS, column]
                target[0, n * SPAN : (n + 1) * SPAN, :] = jnp.where(flip, second, first)
                target[1, n * SPAN : (n + 1) * SPAN, :] = jnp.where(flip, first, second)

        def block(kind, half):
            return kvbuf[kind, :, half, h].reshape(RANKS * SPAN, HEAD)

        def tile(half, i):
            rows = pl.ds(pl.multiple_of(i * ROWS, ROWS), ROWS)
            place_rows = pl.ds(pl.multiple_of(half * WIDTH + i * ROWS, ROWS), ROWS)
            q, g = qs[half, rows, :], gs[half, rows, :]
            scores = [dot_nt(q, block(0, k)) for k in range(half + 1)]
            scores[half] = jnp.where(
                kpos_ref[half : half + 1, :] <= q_pos[half], scores[half], NEG_FILL
            )
            top = jnp.max(scores[0], axis=-1, keepdims=True)
            if half:
                top = jnp.maximum(top, jnp.max(scores[1], axis=-1, keepdims=True))
            weights = [jnp.exp2((s - top) * EXP_SCALE) for s in scores]
            total = jnp.sum(weights[0], axis=-1, keepdims=True)
            if half:
                total = total + jnp.sum(weights[1], axis=-1, keepdims=True)
            low = [w.astype(BF16) for w in weights]
            attended = dot(low[0], block(1, 0))
            if half:
                attended = attended + dot(low[1], block(1, 1))
            share = 1.0 / total
            attended = (attended * share).astype(BF16)
            grad = (g.astype(F32) * (share * SCALE)).astype(BF16)
            grad_f = grad.astype(F32)
            row_dot = jnp.sum(grad_f * attended.astype(F32), axis=-1, keepdims=True)
            gt[:, place_rows] = jnp.transpose(grad_f).astype(BF16)
            qt[:, place_rows] = jnp.transpose(q.astype(F32)).astype(BF16)
            back = None
            for k in range(half + 1):
                dots = dot_nt(grad, block(1, k))
                ds = (weights[k] * (dots - row_dot)).astype(BF16)
                target = rows if k else place_rows
                probs[k, target, :] = low[k]
                dscore[k, target, :] = ds
                term = dot(ds, block(0, k))
                back = term if back is None else back + term
            qs[half, rows, :] = back.astype(BF16)
            gs[half, rows, :] = attended

        def tiles(half, start, stop):
            def body(i, inner):
                tile(half, i)
                return inner

            lax.fori_loop(start, stop, body, 0)

        serve(h - 1, 1)
        tiles(0, 0, 4)
        serve(h - 1, 2)
        tiles(1, 0, 2)
        serve(h - 1, 3)
        tiles(1, 2, 4)
        serve(h - 1, 4)
        for kind, left, right in ((0, qt, dscore), (1, gt, probs)):
            low = dot(left[...], right[0])
            high = dot(left[:, WIDTH:], right[1, 0:WIDTH, :])
            for half, array in ((0, low), (1, high)):
                grads[h, kind, :, half] = (
                    jnp.transpose(array).astype(BF16).reshape(RANKS, SPAN, HEAD)
                )
        for route in scatters(h):
            route.stage(0)
        for n in range(GROUP):
            column = pl.ds(pl.multiple_of((h * GROUP + n) * HEAD, HEAD), HEAD)
            for source, target in ((qs, dq_ref), (gs, out_ref)):
                low = source[0, n * SPAN : (n + 1) * SPAN, :]
                high = source[1, n * SPAN : (n + 1) * SPAN, :]
                target[0:SPAN, column] = jnp.where(flip, high, low)
                target[SPAN:ROWS, column] = jnp.where(flip, low, high)
        return carry

    lax.fori_loop(0, HEADS, one_head, 0)
    for number in range(1, 5):
        serve(jnp.int32(HEADS - 1), number)

    def pair_copy(r):
        return pltpu.make_async_remote_copy(
            src_ref=terms.at[1 - me.core, r],
            dst_ref=pair.at[r],
            send_sem=pair_send.at[r],
            recv_sem=pair_recv.at[r],
            device_id=me.partner(),
            device_id_type=MESH,
        )

    def weight_terms(r, mean):
        unit = unit_piece(r)
        gain = gain_piece(r)
        normed_t = jnp.transpose(unit * gain).astype(BF16)
        dk, dv = dkv[:, 0:WIDTH], dkv[:, WIDTH:]
        terms[0, r, 0:SHARE, :] = dot(normed_t, dk).astype(BF16)
        terms[1, r, 0:SHARE, :] = dot(normed_t, dv).astype(BF16)
        normed_grad = dot_nt(dk, wbuf[0, r, 0:SHARE, :]) + dot_nt(dv, wbuf[1, r, 0:SHARE, :])
        gain_term = jnp.sum(unit * normed_grad, axis=0, keepdims=True)
        for kind in range(2):
            terms[kind, r, SHARE:BLOCK, 0:SHARE] = jnp.broadcast_to(
                gain_term, (16, SHARE)
            ).astype(BF16)
            terms[kind, r, SHARE:BLOCK, SHARE:WIDTH] = jnp.zeros((16, WIDTH - SHARE), BF16)
        pair_copy(r).start()
        unit_grad = normed_grad * gain
        ngrad[:, pl.ds(pl.multiple_of(r * SHARE, SHARE), SHARE)] = unit_grad
        return mean + jnp.sum(unit_grad * unit, axis=-1, keepdims=True)

    mean = lax.fori_loop(0, RANKS, weight_terms, jnp.zeros((ROWS, 1), F32))
    mean = mean * (1.0 / FEATURES)

    def pair_sum(r, carry):
        pair_copy(r).wait()
        terms[me.core, r] = (terms[me.core, r].astype(F32) + pair[r].astype(F32)).astype(BF16)
        return carry

    lax.fori_loop(0, RANKS, pair_sum, 0)

    def half_rows(kind, part):
        return pl.ds(0, 80 if (kind and part == "hi") else 64)

    w_scatters = [
        Scatter(
            me,
            "yz"[kind],
            lambda rank, part, kind=kind: terms.at[me.core, rank, weight_rows(kind, part)],
            lambda i, part, kind=kind: w_half.at[
                kind, i, 0 if part == "lo" else 1, half_rows(kind, part)
            ],
            lambda i, side, kind=kind: w_whole.at[kind, i, side, pl.ds(0, 144 if kind else 128)],
            ws_send.at[kind],
            ws_recv.at[kind],
        )
        for kind in range(2)
    ]
    for route in w_scatters:
        route.stage(0)

    def row_grad(r, carry):
        columns = pl.ds(pl.multiple_of(r * SHARE, SHARE), SHARE)
        dx_ref[:, columns] = (
            inv_ref[...] * (ngrad[:, columns] - unit_piece(r) * mean)
        ).astype(BF16)
        return carry

    lax.fori_loop(0, RANKS, row_grad, 0)
    for number in range(1, 5):
        for route in w_scatters:
            route.stage(number)

    for kind, route in enumerate(w_scatters):
        x_send[128 * kind : 128 * kind + (144 if kind else 128), :] = route.total().astype(BF16)

    def quarter(number):
        return pl.ds(pl.multiple_of(number * 64, 64), 64)

    def x_copy(index, src, dst, to):
        return pltpu.make_async_remote_copy(
            src_ref=src,
            dst_ref=dst,
            send_sem=x_ssem.at[index],
            recv_sem=x_rsem.at[index],
            device_id=to,
            device_id_type=MESH,
        )

    sums = [
        x_copy(d - 1, x_send.at[quarter((me.x + d) % 4)], x_recv.at[d - 1], me.along_x(d))
        for d in (1, 2, 3)
    ]
    gains = [
        x_copy(d + 2, x_send.at[pl.ds(SHARE, 16)], x_gain.at[d - 1], me.along_x(d))
        for d in (1, 2, 3)
    ]
    for copy in sums + gains:
        copy.start()
    for copy in sums:
        copy.wait_recv()
    total = x_send[quarter(me.x), :].astype(F32)
    for d in range(3):
        total = total + x_recv[d].astype(F32)
    final[me.core, quarter(me.x), :] = total.astype(BF16)
    mine = final.at[me.core, quarter(me.x)]
    spread = [x_copy(5 + d, mine, mine, me.along_x(d)) for d in (1, 2, 3)]
    for copy in spread:
        copy.start()
    for copy in gains:
        copy.wait_recv()
    total = x_send[SHARE:BLOCK, :].astype(F32)
    for d in range(3):
        total = total + x_gain[d].astype(F32)
    dgain_ref[...] = total[0:8, 0:SHARE]
    for d in (1, 2, 3):
        theirs = final.at[me.core, quarter((me.x + 4 - d) % 4)]
        x_copy(5 + d, theirs, theirs, me.along_x(d)).wait_recv()
    last = x_copy(9, final.at[me.core], final.at[me.core], me.partner())
    last.start()
    x_copy(9, final.at[1 - me.core], final.at[1 - me.core], me.partner()).wait_recv()
    dwk_ref[...] = final[0].astype(F32)
    dwv_ref[...] = final[1].astype(F32)

    for kind, route in enumerate(w_routes):
        route.drain()
        for block in blocks:
            hand(kind, route, block).wait_send()
    for route in kv_routes:
        route.drain()

    def drain_head(h, carry):
        for route in scatters(h):
            route.drain()
        return carry

    lax.fori_loop(0, HEADS, drain_head, 0)
    for route in w_scatters:
        route.drain()
    for copy in sums + gains + spread + [last]:
        copy.wait_send()


def local(inputs, queries, out_grad, span_ids, norm_gain, key_weight, value_weight):
    rank = lax.axis_index("shard") * 8 + lax.axis_index("ctx")
    spans = span_ids.reshape(RANKS, 2)
    own = lax.dynamic_slice_in_dim(spans, rank, 1, 0).reshape(2, 1)
    token = jnp.arange(SPAN, dtype=jnp.int32)[None, :]
    own_pos = (own * SPAN + token).reshape(ROWS)
    low = jnp.minimum(spans[:, 0], spans[:, 1])[:, None] * SPAN + token
    high = jnp.maximum(spans[:, 0], spans[:, 1])[:, None] * SPAN + token
    kpos = jnp.stack([low.reshape(-1), high.reshape(-1)])
    half = HEAD // 2
    frequency = jnp.exp(
        -math.log(ROPE_BASE) * (2.0 * jnp.arange(half, dtype=jnp.float32) / HEAD)
    )
    angles = own_pos.astype(jnp.float32)[:, None] * frequency[None, :]
    cosine, sine = jnp.cos(angles), jnp.sin(angles)
    cosine = jnp.concatenate([cosine, cosine], axis=1)
    sine = jnp.concatenate([-sine, sine], axis=1)

    vmem = pl.BlockSpec(memory_space=pltpu.VMEM)
    smem = pl.BlockSpec(memory_space=pltpu.SMEM)
    dma = pltpu.SemaphoreType.DMA
    outs = pl.pallas_call(
        kernel,
        out_shape=[
            jax.ShapeDtypeStruct((ROWS, FEATURES), BF16),
            jax.ShapeDtypeStruct((ROWS, FEATURES), BF16),
            jax.ShapeDtypeStruct((ROWS, FEATURES), BF16),
            jax.ShapeDtypeStruct((SHARE, WIDTH), F32),
            jax.ShapeDtypeStruct((SHARE, WIDTH), F32),
            jax.ShapeDtypeStruct((8, SHARE), F32),
        ],
        in_specs=[vmem, vmem, vmem, smem] + [vmem] * 6,
        out_specs=[vmem] * 6,
        scratch_shapes=[
            pltpu.VMEM((2, RANKS, BLOCK, WIDTH), BF16),
            pltpu.VMEM((2, RANKS, 2, HEADS, SPAN, HEAD), BF16),
            pltpu.VMEM((2, WIDTH, HEAD), BF16),
            pltpu.VMEM((2, WIDTH, HEAD), BF16),
            pltpu.VMEM((HEAD, 2 * WIDTH), BF16),
            pltpu.VMEM((HEAD, 2 * WIDTH), BF16),
            pltpu.VMEM((2, 2 * WIDTH, RANKS * SPAN), BF16),
            pltpu.VMEM((2, 2 * WIDTH, RANKS * SPAN), BF16),
            pltpu.VMEM((HEADS, 2, RANKS, 2, SPAN, HEAD), BF16),
            pltpu.VMEM((HEADS, 2, 5, 2, SPAN, HEAD), BF16),
            pltpu.VMEM((HEADS, 2, 5, 2, 2, SPAN, HEAD), BF16),
            pltpu.VMEM((ROWS, 2 * WIDTH), BF16),
            pltpu.VMEM((ROWS, FEATURES), F32),
            pltpu.VMEM((2, RANKS, BLOCK, WIDTH), BF16),
            pltpu.VMEM((RANKS, BLOCK, WIDTH), BF16),
            pltpu.VMEM((2, 5, 2, 80, WIDTH), BF16),
            pltpu.VMEM((2, 5, 2, 144, WIDTH), BF16),
            pltpu.VMEM((BLOCK, WIDTH), BF16),
            pltpu.VMEM((3, 64, WIDTH), BF16),
            pltpu.VMEM((3, 16, WIDTH), BF16),
            pltpu.VMEM((2, SHARE, WIDTH), BF16),
            pltpu.VMEM((ROWS, 1), F32),
            dma((2, 20)), dma((2, 20)),
            dma((2, 16)), dma((2, 16)),
            dma((2, 20)), dma((2, 20)),
            dma((HEADS, 2, 20)), dma((HEADS, 2, 20)),
            dma((RANKS,)), dma((RANKS,)),
            dma((2, 20)), dma((2, 20)),
            dma((10,)), dma((10,)),
        ],
        compiler_params=pltpu.CompilerParams(
            collective_id=0, has_side_effects=True, vmem_limit_bytes=60 * 1024 * 1024
        ),
        cost_estimate=pl.CostEstimate(
            flops=12 * 10**9, bytes_accessed=10**7, transcendentals=7 * 10**6
        ),
        name="layer",
    )(
        inputs, queries, out_grad, spans.reshape(-1), kpos, norm_gain.reshape(1, SHARE),
        key_weight, value_weight, cosine, sine,
    )
    return (*outs[:5], outs[5][0])


def solution(mesh):
    tokens = P(("dp", "shard", "ctx"), None)
    rows = P(("shard", "ctx"), None)
    return jax.shard_map(
        local,
        mesh=mesh,
        in_specs=(tokens, tokens, tokens, P("dp", None, None), P(("shard", "ctx")), rows, rows),
        out_specs=(tokens, tokens, tokens, rows, rows, P(("shard", "ctx"))),
        check_vma=False,
    )
```

```python
import functools
import math

import jax
import jax.numpy as jnp
from jax import lax
from jax.experimental import pallas as pl
from jax.experimental.pallas import tpu as pltpu
from jax.sharding import PartitionSpec as P

HEAD = 128
HEADS = 4
GROUP = 8
SPAN = 64
RANKS = 16
ROWS = 128
FEATURES = 4096
SHARE = 256
WIDTH = 512
BLOCK = 144
PART = 128
EARLY = 2
EPSILON = 1e-05
ROPE_BASE = 500000.0
NEG_FILL = -1e30
SCALE = HEAD ** (-0.5)
EXP_SCALE = SCALE * math.log2(math.e)
MESH = pl.DeviceIdType.MESH
F32 = jnp.float32
BF16 = jnp.bfloat16
NT = (((1,), (1,)), ((), ()))


def device_at(x, core, y, z):
    return (x * 2 + core, z % 2, (z // 2) * 4 + y)


def rank_at(y, z):
    return (z % 2) * 8 + (z // 2) * 4 + y


def dot(a, b):
    return jnp.dot(a, b, preferred_element_type=F32)


def dot_nt(a, b):
    return lax.dot_general(a, b, NT, preferred_element_type=F32)


class Place:
    def __init__(self):
        dp = lax.axis_index("dp")
        shard = lax.axis_index("shard")
        ctx = lax.axis_index("ctx")
        self.x = dp // 2
        self.core = dp % 2
        self.y = ctx % 4
        self.z = (ctx // 4) * 2 + shard
        self.rank = rank_at(self.y, self.z)

    def partner(self):
        return device_at(self.x, 1 - self.core, self.y, self.z)

    def along_x(self, step):
        return device_at((self.x + step) % 4, self.core, self.y, self.z)


STEPS = (1, 3, 2)


def start_all(copies):
    for copy in copies:
        copy.start()


def add_into(ref, others):
    total = ref[...].astype(F32)
    for other in others:
        total = total + other[...].astype(F32)
    ref[...] = total.astype(BF16)


class Route:
    def __init__(self, place, kind, slot, send, recv):
        self.place, self.kind, self.slot = place, kind, slot
        self.send_sems, self.recv_sems = send, recv
        self.a, self.b = (place.z, place.y) if kind else (place.y, place.z)

    def block(self, da, db):
        a, b = (self.a + da) % 4, (self.b + db) % 4
        return self.slot(a, b) if self.kind else self.slot(b, a)

    def column(self, db):
        b = (self.b + db) % 4
        return self.slot(slice(None), b) if self.kind else self.slot(b, slice(None))

    def device(self, da, db):
        a, b = (self.a + da) % 4, (self.b + db) % 4
        y, z = (b, a) if self.kind else (a, b)
        return device_at(self.place.x, self.place.core, y, z)

    def copy(self, index, src, dst, to):
        return pltpu.make_async_remote_copy(
            src_ref=src,
            dst_ref=dst,
            send_sem=self.send_sems.at[index],
            recv_sem=self.recv_sems.at[index],
            device_id=to,
            device_id_type=MESH,
        )

    def drain(self):
        for n in range(6):
            self.message(n).wait_send()


class Gather(Route):
    def message(self, n, back=False):
        step = STEPS[n % 3]
        if n < 3:
            ref = self.block(4 - step if back else 0, 0)
            return self.copy(n, ref, ref, self.device(step, 0))
        ref = self.column(4 - step if back else 0)
        return self.copy(n, ref, ref, self.device(0, step))

    def stage(self, number, arrived=None):
        if number == 0:
            start_all([self.message(n) for n in range(3)])
        elif number == 1:
            for n in range(3):
                self.message(n, True).wait_recv()
            start_all([self.message(n) for n in range(3, 6)])
            if arrived is not None:
                arrived(0)
        else:
            for n in range(3, 6):
                self.message(n, True).wait_recv()
                if arrived is not None:
                    arrived(4 - STEPS[n - 3])


class Scatter(Route):
    def __init__(self, place, kind, slot, columns, blocks, send, recv):
        super().__init__(place, kind, slot, send, recv)
        self.columns, self.blocks = columns, blocks

    def message(self, n):
        step = STEPS[n % 3]
        if n < 3:
            return self.copy(n, self.column(step), self.columns(n), self.device(0, step))
        return self.copy(n, self.block(step, 0), self.blocks(n - 3), self.device(step, 0))

    def stage(self, number):
        if number == 0:
            start_all([self.message(n) for n in range(3)])
        elif number == 1:
            for n in range(3):
                self.message(n).wait_recv()
            for n, step in enumerate(STEPS + (0,)):
                place = (self.a + step) % 4
                add_into(self.block(step, 0), [self.columns(i).at[place] for i in range(3)])
                if step:
                    self.message(3 + n).start()
        else:
            for n in range(3, 6):
                self.message(n).wait_recv()

    def total(self):
        total = self.block(0, 0)[...].astype(F32)
        for n in range(3):
            total = total + self.blocks(n)[...].astype(F32)
        return total


class Ring(Route):
    def __init__(self, place, slot, send, recv, landing=None):
        self.place, self.slot, self.send_sems, self.recv_sems = place, slot, send, recv
        self.landing = landing

    def own(self, step):
        return self.slot((self.place.x + step) % 4)

    def drain(self):
        for n in range(3):
            self.message(n).wait_send()


class RingGather(Ring):
    def message(self, n, back=False):
        ref = self.own(4 - STEPS[n] if back else 0)
        return self.copy(n, ref, ref, self.place.along_x(STEPS[n]))

    def stage(self, number):
        if number == 0:
            start_all([self.message(n) for n in range(3)])
        else:
            for n in range(3):
                self.message(n, True).wait_recv()


class RingScatter(Ring):
    def message(self, n):
        return self.copy(n, self.own(STEPS[n]), self.landing(n), self.place.along_x(STEPS[n]))

    def stage(self, number):
        if number == 0:
            start_all([self.message(n) for n in range(3)])
        else:
            for n in range(3):
                self.message(n).wait_recv()
            add_into(self.own(0), [self.landing(n) for n in range(3)])


def tall_rows(kind, with_gain):
    return pl.ds(64, 80 if with_gain else 64) if kind else pl.ds(0, 64)


def piece_rows(number):
    return pl.ds(pl.multiple_of(number * 32, 32), 32)


def kernel(
    x_hbm, q_hbm, g_hbm, spans_ref, kpos_ref, gain_ref, wk_ref, wv_ref, cos_ref, sin_ref,
    out_hbm, dq_hbm, dx_hbm, dwk_ref, dwv_ref, dgain_ref,
    x_ref, q_ref, g_ref, w_first, w_rest, kvbuf, qs, gs, qt, gt, probs_low, probs_high, ds_low, ds_high,
    grads, kv_columns, kv_blocks, dkv, ngrad, normed_t, t_last, p_last, p_rest, q_columns, q_blocks,
    w_columns, w_blocks, r_land, l_land, x_send, x_gain, final, inv_ref,
    io_sem, w_send, w_recv, hand_send, hand_recv, wx_send, wx_recv, kv_send, kv_recv,
    rs_send, rs_recv, pair_send, pair_recv, ws_send, ws_recv, xr_send, xr_recv, x_ssem, x_rsem,
):
    me = Place()

    def wref(h):
        return w_rest.at[h - 1] if h else w_first

    def tref(h):
        return wref(h) if h < HEADS - 1 else t_last

    def pref(h):
        return p_rest.at[h] if h < HEADS - 1 else p_last

    barrier = pltpu.get_barrier_semaphore()
    loads = [
        pltpu.make_async_copy(src, dst, io_sem.at[n])
        for n, (src, dst) in enumerate(((x_hbm, x_ref), (q_hbm, q_ref), (g_hbm, g_ref)))
    ]
    for copy in loads:
        copy.start()

    for h in range(HEADS):
        columns = slice(h * HEAD, (h + 1) * HEAD)
        for part in range(2):
            rows = slice(part * PART, (part + 1) * PART)
            wref(h)[me.z, me.y, part, 0:PART, 0:HEAD] = wk_ref[rows, columns]
            wref(h)[me.z, me.y, part, 0:PART, HEAD : 2 * HEAD] = wv_ref[rows, columns]
    for part in range(2):
        w_first[me.z, me.y, part, PART:BLOCK, :] = jnp.broadcast_to(gain_ref[...], (16, SHARE))

    others = [device_at(me.x, me.core, (me.y + d) % 4, me.z) for d in (1, 2, 3)]
    others += [device_at(me.x, me.core, me.y, (me.z + d) % 4) for d in (1, 2, 3)]
    others += [me.along_x(d) for d in (1, 2, 3)] + [me.partner()]
    for other in others:
        pl.semaphore_signal(barrier, inc=1, device_id=other, device_id_type=MESH)
    pl.semaphore_wait(barrier, len(others))

    w_routes = [
        [
            Gather(
                me,
                kind,
                lambda z, y, h=h, kind=kind: wref(h).at[z, y, me.core, tall_rows(kind, h == 0)],
                w_send.at[h, kind],
                w_recv.at[h, kind],
            )
            for kind in range(2)
        ]
        for h in range(EARLY)
    ]

    late_routes = [
        Gather(
            me,
            kind,
            lambda z, y, kind=kind: w_rest.at[
                pl.ds(EARLY - 1, HEADS - EARLY), z, y, me.core, piece_rows(me.x), pl.ds(kind * HEAD, HEAD)
            ],
            w_send.at[EARLY, kind],
            w_recv.at[EARLY, kind],
        )
        for kind in range(2)
    ]
    for route in late_routes:
        route.column = lambda db, route=route: w_rest.at[
            (pl.ds(EARLY - 1, HEADS - EARLY),)
            + ((slice(None), (route.b + db) % 4) if route.kind else ((route.b + db) % 4, slice(None)))
            + (me.core, piece_rows(me.x), pl.ds(route.kind * HEAD, HEAD))
        ]
    wx = {
        h: RingGather(
            me,
            lambda number, h=h: wref(h).at[:, :, me.core, piece_rows(number)],
            wx_send.at[h - EARLY],
            wx_recv.at[h - EARLY],
        )
        for h in range(EARLY, HEADS)
    }

    def hand_copy(index, ref):
        return pltpu.make_async_remote_copy(
            src_ref=ref,
            dst_ref=ref,
            send_sem=hand_send.at[index],
            recv_sem=hand_recv.at[index],
            device_id=me.partner(),
            device_id_type=MESH,
        )

    def hand_column(core, kind, db):
        b = (w_routes[0][kind].b + db) % 4
        z, y = (slice(None), b) if kind else (b, slice(None))
        return hand_copy(4 * kind + db, w_first.at[z, y, core, tall_rows(kind, True)])

    def hand_head(core, h):
        return hand_copy(7 + h, wref(h).at[:, :, core])

    def w_stage(h, number):
        for kind, route in enumerate(w_routes[h]):
            if h:
                route.stage(number)
            else:
                route.stage(number, lambda db, kind=kind: hand_column(me.core, kind, db).start())
        if h and number == 2:
            hand_head(me.core, h).start()

    def late_stage(number):
        for route in late_routes:
            route.stage(number)

    kv_routes = [
        [
            Gather(
                me,
                kind,
                lambda z, y, h=h, kind=kind: kvbuf.at[h, kind, z, y],
                kv_send.at[h, kind],
                kv_recv.at[h, kind],
            )
            for kind in range(2)
        ]
        for h in range(HEADS)
    ]

    def kv_stage(h, number):
        for route in kv_routes[h]:
            route.stage(number)

    rs_routes = [
        [
            Scatter(
                me,
                kind,
                lambda z, y, h=h, kind=kind: grads.at[h, kind, z, y],
                lambda n, h=h, kind=kind: kv_columns.at[h, kind, n],
                lambda n, h=h, kind=kind: kv_blocks.at[h, kind, n],
                rs_send.at[h, kind],
                rs_recv.at[h, kind],
            )
            for kind in range(2)
        ]
        for h in range(HEADS)
    ]

    first_span = spans_ref[2 * me.rank]
    second_span = spans_ref[2 * me.rank + 1]
    flip = first_span > second_span
    low_span = jnp.minimum(first_span, second_span)
    high_span = jnp.maximum(first_span, second_span)

    def rs_stage(h, number):
        for kind, route in enumerate(rs_routes[h]):
            route.stage(number)
            if number < 2:
                continue
            total = route.total()
            low, high = total[0], total[1]
            total = jnp.concatenate(
                [jnp.where(flip, high, low), jnp.where(flip, low, high)], axis=0
            )
            if kind == 0:
                total = total * cos_ref[...] - pltpu.roll(total, HEAD // 2, 1) * sin_ref[...]
            else:
                total = total * (1.0 / SCALE)
            dkv[h, :, kind * HEAD : (kind + 1) * HEAD] = total.astype(BF16)

    def term_rows(h):
        return pl.ds(0, BLOCK if h == HEADS - 1 else PART)

    def pair_copy(h, j):
        return pltpu.make_async_remote_copy(
            src_ref=tref(h).at[j, :, 1 - me.core, term_rows(h)],
            dst_ref=pref(h).at[j],
            send_sem=pair_send.at[h, j],
            recv_sem=pair_recv.at[h, j],
            device_id=me.partner(),
            device_id_type=MESH,
        )

    def pair_sum(h):
        def group(j, carry):
            pair_copy(h, j).wait_recv()

            def one(n, inner):
                add_into(tref(h).at[j, n, me.core, term_rows(h)], [pref(h).at[j, n]])
                return inner

            lax.fori_loop(0, 4, one, 0)
            return carry

        lax.fori_loop(0, 4, group, 0)

    xr_routes = [
        RingScatter(
            me,
            lambda number, h=h: tref(h).at[:, :, me.core, piece_rows(number)],
            xr_send.at[h],
            xr_recv.at[h],
            lambda n, h=h: r_land.at[h, n],
        )
        for h in range(HEADS - 1)
    ]
    xr_routes.append(
        RingScatter(
            me,
            lambda number: x_send.at[piece_rows(number)],
            xr_send.at[HEADS - 1],
            xr_recv.at[HEADS - 1],
            lambda n: l_land.at[n],
        )
    )
    ws_routes = [
        [
            Scatter(
                me,
                kind,
                lambda z, y, h=h, kind=kind: tref(h).at[
                    z, y, me.core, piece_rows(me.x), pl.ds(kind * HEAD, HEAD)
                ],
                lambda n, h=h, kind=kind: q_columns.at[h, kind, n],
                lambda n, h=h, kind=kind: q_blocks.at[h, kind, n],
                ws_send.at[h, kind],
                ws_recv.at[h, kind],
            )
            for kind in range(2)
        ]
        for h in range(HEADS - 1)
    ]
    ws_routes.append(
        [
            Scatter(
                me,
                kind,
                lambda z, y, kind=kind: t_last.at[z, y, me.core, tall_rows(kind, True)],
                lambda n, kind=kind: w_columns.at[kind, n, :, pl.ds(0, 80 if kind else 64)],
                lambda n, kind=kind: w_blocks.at[kind, n, pl.ds(0, 80 if kind else 64)],
                ws_send.at[HEADS - 1, kind],
                ws_recv.at[HEADS - 1, kind],
            )
            for kind in range(2)
        ]
    )

    def xr_stage(h, number):
        xr_routes[h].stage(number)

    def ws_stage(h, number):
        for kind, route in enumerate(ws_routes[h]):
            route.stage(number)
            if number < 2:
                continue
            total = route.total().astype(BF16)
            if h < HEADS - 1:
                final[
                    me.core, h, piece_rows(me.x), kind * HEAD : (kind + 1) * HEAD
                ] = total
            else:
                x_send[64 * kind : 64 * kind + (80 if kind else 64), :] = total

    def columns_of(r):
        return pl.ds(pl.multiple_of(rank_at(r % 4, r // 4) * SHARE, SHARE), SHARE)

    def unit_piece(r):
        return x_ref[:, columns_of(r)].astype(F32) * inv_ref[...]

    def gain_piece(r):
        return w_first[r // 4, r % 4, 0, PART:BLOCK, :].astype(F32)[0:1, :]

    def weight_block(h, r):
        return wref(h)[r // 4, r % 4, :, 0:PART, :].reshape(SHARE, 2 * HEAD)

    def normalise():
        squares = jnp.zeros((ROWS, HEAD), F32)
        for c in range(FEATURES // HEAD):
            piece = x_ref[:, c * HEAD : (c + 1) * HEAD].astype(F32)
            squares = squares + piece * piece
        inv_ref[...] = lax.rsqrt(
            jnp.sum(squares, axis=-1, keepdims=True) * (1.0 / FEATURES) + EPSILON
        )

    def normed_piece(r):
        return unit_piece(r) * gain_piece(r)

    def turn():
        def one(r, carry):
            normed_t[r] = jnp.transpose(normed_piece(r)).astype(BF16)
            return carry

        lax.fori_loop(0, RANKS, one, 0)

    def project(h):
        raw = lax.fori_loop(
            0,
            RANKS,
            lambda r, total: total + dot(normed_piece(r).astype(BF16), weight_block(h, r)),
            jnp.zeros((ROWS, 2 * HEAD), F32),
        )
        key = raw[:, 0:HEAD]
        key = key * cos_ref[...] + pltpu.roll(key, HEAD // 2, 1) * sin_ref[...]
        for kind, array in ((0, key), (1, raw[:, HEAD:])):
            kvbuf[h, kind, me.z, me.y, 0] = jnp.where(flip, array[SPAN:], array[:SPAN]).astype(BF16)
            kvbuf[h, kind, me.z, me.y, 1] = jnp.where(flip, array[:SPAN], array[SPAN:]).astype(BF16)

    def weight_terms(h):
        last = h == HEADS - 1

        def one(j, n, mean):
            r = 4 * j + n
            grad = dkv[h]
            back = dot_nt(grad, weight_block(h, r))
            block = dot(normed_t[r], grad).astype(BF16)
            tref(h)[j, n, 0, 0:PART, :] = block[0:PART]
            tref(h)[j, n, 1, 0:PART, :] = block[PART:]
            if h:
                back = back + ngrad[:, columns_of(r)]
            if last:
                unit = unit_piece(r)
                gain = jnp.sum(unit * back, axis=0, keepdims=True)
                for part in range(2):
                    t_last[j, n, part, PART:BLOCK, :] = jnp.broadcast_to(gain, (16, SHARE)).astype(
                        BF16
                    )
                back = back * gain_piece(r)
                mean = mean + jnp.sum(back * unit, axis=-1, keepdims=True)
            ngrad[:, columns_of(r)] = back
            return mean

        def group(j, mean):
            mean = lax.fori_loop(0, 4, lambda n, inner: one(j, n, inner), mean)
            pair_copy(h, j).start()
            return mean

        return lax.fori_loop(0, 4, group, jnp.zeros((ROWS, 1), F32))

    token = lax.broadcasted_iota(jnp.int32, (WIDTH, 1), 0) % SPAN
    q_pos = (low_span * SPAN + token, high_span * SPAN + token)

    def load_head(h):
        for n in range(GROUP):
            column = pl.ds(pl.multiple_of((h * GROUP + n) * HEAD, HEAD), HEAD)
            for source, target in ((q_ref, qs), (g_ref, gs)):
                first, second = source[0:SPAN, column], source[SPAN:ROWS, column]
                target[0, n * SPAN : (n + 1) * SPAN, :] = jnp.where(flip, second, first)
                target[1, n * SPAN : (n + 1) * SPAN, :] = jnp.where(flip, first, second)

    def store_head(h):
        for n in range(GROUP):
            column = pl.ds(pl.multiple_of((h * GROUP + n) * HEAD, HEAD), HEAD)
            for source, target in ((qs, q_ref), (gs, g_ref)):
                low = source[0, n * SPAN : (n + 1) * SPAN, :]
                high = source[1, n * SPAN : (n + 1) * SPAN, :]
                target[0:SPAN, column] = jnp.where(flip, high, low)
                target[SPAN:ROWS, column] = jnp.where(flip, low, high)

    def attend(h, half):
        def block(kind, side):
            return kvbuf[h, kind, :, :, side].reshape(RANKS * SPAN, HEAD)

        place_rows = slice(half * WIDTH, (half + 1) * WIDTH)
        q, g = qs[half], gs[half]
        scores = [dot_nt(q, block(0, k)) for k in range(half + 1)]
        scores[half] = jnp.where(
            kpos_ref[half : half + 1, :] <= q_pos[half], scores[half], NEG_FILL
        )
        top = jnp.max(scores[0], axis=-1, keepdims=True)
        if half:
            top = jnp.maximum(top, jnp.max(scores[1], axis=-1, keepdims=True))
        weights = [jnp.exp2((s - top) * EXP_SCALE) for s in scores]
        total = jnp.sum(weights[0], axis=-1, keepdims=True)
        if half:
            total = total + jnp.sum(weights[1], axis=-1, keepdims=True)
        low = [w.astype(BF16) for w in weights]
        attended = dot(low[0], block(1, 0))
        if half:
            attended = attended + dot(low[1], block(1, 1))
        share = 1.0 / total
        attended = (attended * share).astype(BF16)
        grad = (g.astype(F32) * (share * SCALE)).astype(BF16)
        grad_f = grad.astype(F32)
        row_dot = jnp.sum(grad_f * attended.astype(F32), axis=-1, keepdims=True)
        gt[:, place_rows] = jnp.transpose(grad_f).astype(BF16)
        qt[:, place_rows] = jnp.transpose(q.astype(F32)).astype(BF16)
        back = None
        for k in range(half + 1):
            dots = dot_nt(grad, block(1, k))
            ds = (low[k].astype(F32) * (dots - row_dot)).astype(BF16)
            if k:
                probs_high[...] = low[k]
                ds_high[...] = ds
            else:
                probs_low[place_rows, :] = low[k]
                ds_low[place_rows, :] = ds
            term = dot(ds, block(0, k))
            back = term if back is None else back + term
        qs[half] = back.astype(BF16)
        gs[half] = attended

    def key_terms(h):
        for kind, left, low, high in ((0, qt, ds_low, ds_high), (1, gt, probs_low, probs_high)):
            for side, array in (
                (0, dot(left[...], low[...])),
                (1, dot(left[:, WIDTH:], high[...])),
            ):
                grads[h, kind, :, :, side] = (
                    jnp.transpose(array).astype(BF16).reshape(4, 4, SPAN, HEAD)
                )

    w_stage(0, 0)
    w_stage(1, 0)
    late_stage(0)
    loads[0].wait()
    normalise()
    w_stage(0, 1)
    w_stage(1, 1)
    late_stage(1)
    w_stage(0, 2)
    for kind in range(2):
        for db in range(4):
            hand_column(1 - me.core, kind, db).wait_recv()
    project(0)
    kv_stage(0, 0)
    w_stage(1, 2)
    turn()
    kv_stage(0, 1)
    hand_head(1 - me.core, 1).wait_recv()
    project(1)
    kv_stage(1, 0)
    late_stage(2)
    wx[2].stage(0)
    wx[3].stage(0)
    loads[1].wait()
    loads[2].wait()
    kv_stage(0, 2)

    def late_projection(h):
        hand_head(1 - me.core, h).wait_recv()
        project(h)
        kv_stage(h, 0)

    def late_arrival(h):
        wx[h].stage(1)
        hand_head(me.core, h).start()

    def xr_begin(h):
        pair_sum(h)
        xr_stage(h, 0)

    def xr_end(h):
        xr_stage(h, 1)
        ws_stage(h, 0)

    def weights_left():
        for routes in w_routes + [late_routes]:
            for route in routes:
                route.drain()
        for route in wx.values():
            route.drain()
        for kind in range(2):
            for db in range(4):
                hand_column(me.core, kind, db).wait_send()
        for h in range(1, HEADS):
            hand_head(me.core, h).wait_send()

    plan = {
        (0, 0): [lambda: kv_stage(1, 1)],
        (0, 2): [lambda: late_arrival(2), lambda: kv_stage(1, 2)],
        (0, 3): [lambda: rs_stage(0, 0)],
        (0, 4): [lambda: late_projection(2)],
        (1, 1): [lambda: kv_stage(2, 1), lambda: rs_stage(0, 1)],
        (1, 2): [lambda: late_arrival(3), lambda: rs_stage(0, 2), lambda: kv_stage(2, 2)],
        (1, 3): [lambda: rs_stage(1, 0)],
        (1, 4): [lambda: late_projection(3), weights_left, lambda: weight_terms(0)],
        (2, 0): [lambda: kv_stage(3, 1)],
        (2, 1): [lambda: rs_stage(1, 1), lambda: xr_begin(0)],
        (2, 2): [lambda: kv_stage(3, 2), lambda: rs_stage(1, 2)],
        (2, 3): [lambda: rs_stage(2, 0)],
        (2, 4): [lambda: weight_terms(1)],
        (3, 1): [lambda: rs_stage(2, 1), lambda: xr_end(0), lambda: xr_begin(1)],
        (3, 2): [lambda: rs_stage(2, 2), lambda: ws_stage(0, 1)],
        (3, 3): [lambda: rs_stage(3, 0)],
        (3, 4): [lambda: weight_terms(2), lambda: ws_stage(0, 2), lambda: xr_end(1)],
    }

    def one_head(h, carry):
        def serve(point):
            for head in range(HEADS):
                if (head, point) not in plan:
                    continue

                @pl.when(h == head)
                def _():
                    for item in plan[head, point]:
                        item()

        load_head(h)
        serve(0)
        attend(h, 0)
        serve(1)
        attend(h, 1)
        serve(2)
        key_terms(h)
        serve(3)
        store_head(h)
        serve(4)
        return carry

    lax.fori_loop(0, HEADS, one_head, 0)

    stores = [
        pltpu.make_async_copy(g_ref, out_hbm, io_sem.at[0]),
        pltpu.make_async_copy(q_ref, dq_hbm, io_sem.at[1]),
    ]
    for copy in stores:
        copy.start()

    def x_copy(index, ref, dst, to):
        return pltpu.make_async_remote_copy(
            src_ref=ref,
            dst_ref=dst,
            send_sem=x_ssem.at[index],
            recv_sem=x_rsem.at[index],
            device_id=to,
            device_id_type=MESH,
        )

    def spread(base, heads, d, owner):
        ref = final.at[me.core, heads, piece_rows(owner)]
        return x_copy(base + d - 1, ref, ref, me.along_x(d))

    def to_partner(index, heads, core):
        ref = final.at[core, heads]
        return x_copy(index, ref, ref, me.partner())

    def spread_start(base, heads):
        for d in (1, 2, 3):
            spread(base, heads, d, me.x).start()

    def spread_wait(base, heads):
        for d in (1, 2, 3):
            spread(base, heads, d, (me.x + 4 - d) % 4).wait_recv()

    early_heads, late_head = pl.ds(0, HEADS - 1), pl.ds(HEADS - 1, 1)
    rs_stage(3, 1)
    xr_begin(2)
    ws_stage(1, 1)
    rs_stage(3, 2)
    mean = weight_terms(3) * (1.0 / FEATURES)
    pair_sum(3)
    ws_stage(3, 0)
    ws_stage(1, 2)
    xr_end(2)

    def row_grad(r, carry):
        dx = inv_ref[...] * (ngrad[:, columns_of(r)] - unit_piece(r) * mean)
        x_ref[:, columns_of(r)] = dx.astype(BF16)
        return carry

    lax.fori_loop(0, RANKS, row_grad, 0)
    stores.append(pltpu.make_async_copy(x_ref, dx_hbm, io_sem.at[2]))
    stores[2].start()
    ws_stage(3, 1)
    ws_stage(2, 1)
    ws_stage(3, 2)
    xr_stage(3, 0)
    gains = [
        x_copy(5 + d, x_send.at[pl.ds(PART, 16)], x_gain.at[d - 1], me.along_x(d))
        for d in (1, 2, 3)
    ]
    for copy in gains:
        copy.start()
    ws_stage(2, 2)
    spread_start(0, early_heads)
    xr_stage(3, 1)
    final[me.core, HEADS - 1, piece_rows(me.x)] = x_send[piece_rows(me.x), :]
    spread_start(3, late_head)
    spread_wait(0, early_heads)
    to_partner(9, early_heads, me.core).start()
    for copy in gains:
        copy.wait_recv()
    total = x_send[PART:BLOCK, :].astype(F32)
    for d in range(3):
        total = total + x_gain[d].astype(F32)
    dgain_ref[...] = total[0:8, :]
    spread_wait(3, late_head)
    to_partner(10, late_head, me.core).start()

    def write_weights(heads):
        for h in heads:
            for core in range(2):
                rows, columns = slice(core * PART, (core + 1) * PART), slice(h * HEAD, (h + 1) * HEAD)
                dwk_ref[rows, columns] = final[core, h, :, 0:HEAD].astype(F32)
                dwv_ref[rows, columns] = final[core, h, :, HEAD:].astype(F32)

    to_partner(9, early_heads, 1 - me.core).wait_recv()
    write_weights(range(HEADS - 1))
    to_partner(10, late_head, 1 - me.core).wait_recv()
    write_weights((HEADS - 1,))

    for routes in kv_routes + rs_routes + ws_routes:
        for route in routes:
            route.drain()
    for route in xr_routes:
        route.drain()
    for h in range(HEADS):
        for j in range(4):
            pair_copy(h, j).wait_send()
    for copy in gains:
        copy.wait_send()
    for base, heads in ((0, early_heads), (3, late_head)):
        for d in (1, 2, 3):
            spread(base, heads, d, me.x).wait_send()
    to_partner(9, early_heads, me.core).wait_send()
    to_partner(10, late_head, me.core).wait_send()
    for copy in stores:
        copy.wait()


def settle(*refs):
    count = len(refs) // 2
    for n in range(count):
        refs[count + n][...] = refs[n][...]


def local(inputs, queries, out_grad, span_ids, norm_gain, key_weight, value_weight):
    rank = lax.axis_index("shard") * 8 + lax.axis_index("ctx")
    spans = span_ids.reshape(RANKS, 2)
    own = lax.dynamic_slice_in_dim(spans, rank, 1, 0).reshape(2, 1)
    token = jnp.arange(SPAN, dtype=jnp.int32)[None, :]
    own_pos = (own * SPAN + token).reshape(ROWS)
    ordered = spans.reshape(2, 2, 4, 2).transpose(1, 0, 2, 3).reshape(RANKS, 2)
    low = jnp.minimum(ordered[:, 0], ordered[:, 1])[:, None] * SPAN + token
    high = jnp.maximum(ordered[:, 0], ordered[:, 1])[:, None] * SPAN + token
    kpos = jnp.stack([low.reshape(-1), high.reshape(-1)])
    half = HEAD // 2
    frequency = jnp.exp(
        -math.log(ROPE_BASE) * (2.0 * jnp.arange(half, dtype=jnp.float32) / HEAD)
    )
    angles = own_pos.astype(jnp.float32)[:, None] * frequency[None, :]
    cosine, sine = jnp.cos(angles), jnp.sin(angles)
    cosine = jnp.concatenate([cosine, cosine], axis=1)
    sine = jnp.concatenate([-sine, sine], axis=1)

    vmem = pl.BlockSpec(memory_space=pltpu.VMEM)
    smem = pl.BlockSpec(memory_space=pltpu.SMEM)
    anywhere = pl.BlockSpec(memory_space=pl.ANY)
    dma = pltpu.SemaphoreType.DMA
    outs = pl.pallas_call(
        kernel,
        out_shape=[
            jax.ShapeDtypeStruct((ROWS, FEATURES), BF16),
            jax.ShapeDtypeStruct((ROWS, FEATURES), BF16),
            jax.ShapeDtypeStruct((ROWS, FEATURES), BF16),
            jax.ShapeDtypeStruct((SHARE, WIDTH), F32),
            jax.ShapeDtypeStruct((SHARE, WIDTH), F32),
            jax.ShapeDtypeStruct((8, SHARE), F32),
        ],
        in_specs=[anywhere] * 3 + [smem] + [vmem] * 6,
        out_specs=[anywhere] * 3 + [vmem] * 3,
        scratch_shapes=[
            pltpu.VMEM((ROWS, FEATURES), BF16),
            pltpu.VMEM((ROWS, FEATURES), BF16),
            pltpu.VMEM((ROWS, FEATURES), BF16),
            pltpu.VMEM((4, 4, 2, BLOCK, 2 * HEAD), BF16),
            pltpu.VMEM((HEADS - 1, 4, 4, 2, PART, 2 * HEAD), BF16),
            pltpu.VMEM((HEADS, 2, 4, 4, 2, SPAN, HEAD), BF16),
            pltpu.VMEM((2, WIDTH, HEAD), BF16),
            pltpu.VMEM((2, WIDTH, HEAD), BF16),
            pltpu.VMEM((HEAD, 2 * WIDTH), BF16),
            pltpu.VMEM((HEAD, 2 * WIDTH), BF16),
            pltpu.VMEM((2 * WIDTH, RANKS * SPAN), BF16),
            pltpu.VMEM((WIDTH, RANKS * SPAN), BF16),
            pltpu.VMEM((2 * WIDTH, RANKS * SPAN), BF16),
            pltpu.VMEM((WIDTH, RANKS * SPAN), BF16),
            pltpu.VMEM((HEADS, 2, 4, 4, 2, SPAN, HEAD), BF16),
            pltpu.VMEM((HEADS, 2, 3, 4, 2, SPAN, HEAD), BF16),
            pltpu.VMEM((HEADS, 2, 3, 2, SPAN, HEAD), BF16),
            pltpu.VMEM((HEADS, ROWS, 2 * HEAD), BF16),
            pltpu.VMEM((ROWS, FEATURES), F32),
            pltpu.VMEM((RANKS, SHARE, ROWS), BF16),
            pltpu.VMEM((4, 4, 2, BLOCK, 2 * HEAD), BF16),
            pltpu.VMEM((4, 4, BLOCK, 2 * HEAD), BF16),
            pltpu.VMEM((HEADS - 1, 4, 4, PART, 2 * HEAD), BF16),
            pltpu.VMEM((HEADS - 1, 2, 3, 4, 32, HEAD), BF16),
            pltpu.VMEM((HEADS - 1, 2, 3, 32, HEAD), BF16),
            pltpu.VMEM((2, 3, 4, 80, 2 * HEAD), BF16),
            pltpu.VMEM((2, 3, 80, 2 * HEAD), BF16),
            pltpu.VMEM((HEADS - 1, 3, 4, 4, 32, 2 * HEAD), BF16),
            pltpu.VMEM((3, 32, 2 * HEAD), BF16),
            pltpu.VMEM((BLOCK, 2 * HEAD), BF16),
            pltpu.VMEM((3, 16, 2 * HEAD), BF16),
            pltpu.VMEM((2, HEADS, PART, 2 * HEAD), BF16),
            pltpu.VMEM((ROWS, 1), F32),
            dma((3,)),
            dma((EARLY + 1, 2, 6)), dma((EARLY + 1, 2, 6)),
            dma((7 + HEADS,)), dma((7 + HEADS,)),
            dma((HEADS - EARLY, 3)), dma((HEADS - EARLY, 3)),
            dma((HEADS, 2, 6)), dma((HEADS, 2, 6)),
            dma((HEADS, 2, 6)), dma((HEADS, 2, 6)),
            dma((HEADS, 4)), dma((HEADS, 4)),
            dma((HEADS, 2, 6)), dma((HEADS, 2, 6)),
            dma((HEADS, 3)), dma((HEADS, 3)),
            dma((11,)), dma((11,)),
        ],
        compiler_params=pltpu.CompilerParams(
            collective_id=0, has_side_effects=True, vmem_limit_bytes=55 * 1024 * 1024
        ),
        cost_estimate=pl.CostEstimate(
            flops=12 * 10**9, bytes_accessed=10**7, transcendentals=7 * 10**6
        ),
        name="layer",
    )(
        inputs, queries, out_grad, spans.reshape(-1), kpos, norm_gain.reshape(1, SHARE),
        key_weight, value_weight, cosine, sine,
    )
    blocks = [pl.BlockSpec((ROWS, FEATURES // 4), lambda i: (0, i))] * 3
    blocks += [pl.BlockSpec((SHARE // 4, WIDTH), lambda i: (i, 0))] * 2
    blocks += [pl.BlockSpec((8, SHARE), lambda i: (0, 0))]
    outs = pl.pallas_call(
        settle,
        out_shape=[jax.ShapeDtypeStruct(o.shape, o.dtype) for o in outs],
        grid=(4,),
        in_specs=blocks,
        out_specs=blocks,
        name="settle",
    )(*outs)
    return (*outs[:5], outs[5][0])


def solution(mesh):
    tokens = P(("dp", "shard", "ctx"), None)
    rows = P(("shard", "ctx"), None)
    return jax.shard_map(
        local,
        mesh=mesh,
        in_specs=(tokens, tokens, tokens, P("dp", None, None), P(("shard", "ctx")), rows, rows),
        out_specs=(tokens, tokens, tokens, rows, rows, P(("shard", "ctx"))),
        check_vma=False,
    )
```

```python
import functools
import math

import jax
import jax.numpy as jnp
import numpy as np
from jax import lax
from jax.experimental import pallas as pl
from jax.experimental.pallas import tpu as pltpu
from jax.sharding import PartitionSpec as P

HEAD = 128
HEADS = 4
GROUP = 8
SPAN = 64
RANKS = 16
ROWS = 128
FEATURES = 4096
SHARE = 256
WIDTH = 512
BLOCK = 144
FOUR = 1024
PART = 128
EARLY = 1
EPSILON = 1e-05
ROPE_BASE = 500000.0
NEG_FILL = -1e30
SCALE = HEAD ** (-0.5)
EXP_SCALE = SCALE * math.log2(math.e)
MESH = pl.DeviceIdType.MESH
F32 = jnp.float32
BF16 = jnp.bfloat16
NT = (((1,), (1,)), ((), ()))


def device_at(x, core, y, z):
    return (x * 2 + core, z % 2, (z // 2) * 4 + y)


def rank_at(y, z):
    return (z % 2) * 8 + (z // 2) * 4 + y


def dot(a, b):
    return jnp.dot(a, b, preferred_element_type=F32)


def dot_nt(a, b):
    return lax.dot_general(a, b, NT, preferred_element_type=F32)


class Place:
    def __init__(self):
        dp = lax.axis_index("dp")
        shard = lax.axis_index("shard")
        ctx = lax.axis_index("ctx")
        self.x = dp // 2
        self.core = dp % 2
        self.y = ctx % 4
        self.z = (ctx // 4) * 2 + shard
        self.rank = rank_at(self.y, self.z)

    def partner(self):
        return device_at(self.x, 1 - self.core, self.y, self.z)

    def along_x(self, step):
        return device_at((self.x + step) % 4, self.core, self.y, self.z)


STEPS = (1, 3, 2)


def start_all(copies):
    for copy in copies:
        copy.start()


def add_into(ref, others):
    total = ref[...].astype(F32)
    for other in others:
        total = total + other[...].astype(F32)
    ref[...] = total.astype(BF16)


class Route:
    def __init__(self, place, kind, slot, half, send, recv):
        self.place, self.kind, self.slot, self.half = place, kind, slot, half
        self.send_sems, self.recv_sems = send, recv
        self.a, self.b = (place.z, place.y) if kind else (place.y, place.z)

    def block(self, da, db):
        a, b = (self.a + da) % 4, (self.b + db) % 4
        return self.slot(a, b) if self.kind else self.slot(b, a)

    def column(self, db):
        b = (self.b + db) % 4
        return self.slot(slice(None), b) if self.kind else self.slot(b, slice(None))

    def device(self, da, db):
        a, b = (self.a + da) % 4, (self.b + db) % 4
        y, z = (b, a) if self.kind else (a, b)
        return device_at(self.place.x, self.place.core, y, z)

    def copy(self, index, src, dst, to):
        return pltpu.make_async_remote_copy(
            src_ref=src,
            dst_ref=dst,
            send_sem=self.send_sems.at[index],
            recv_sem=self.recv_sems.at[index],
            device_id=to,
            device_id_type=MESH,
        )

    def drain(self):
        for n in range(7):
            self.message(n).wait_send()


class Gather(Route):
    def message(self, n, back=False):
        if n < 3:
            ref = self.block(4 - STEPS[n] if back else 0, 0)
            return self.copy(n, ref, ref, self.device(STEPS[n], 0))
        step = 1 if n % 2 else 3
        if n < 5:
            ref = self.column(4 - step if back else 0)
        else:
            ref = self.half(self.column(2 if back else 4 - step), n - 5)
        return self.copy(n, ref, ref, self.device(0, step))

    def stage(self, number, arrived=lambda db: None):
        if number == 0:
            start_all([self.message(n) for n in range(3)])
        elif number == 1:
            for n in range(3):
                self.message(n, True).wait_recv()
            start_all([self.message(n) for n in (3, 4)])
            arrived(0)
        elif number == 2:
            for n, db in ((3, 3), (4, 1)):
                self.message(n, True).wait_recv()
                self.message(n + 2).start()
                arrived(db)
        else:
            for n in (5, 6):
                self.message(n, True).wait_recv()
            arrived(2)


class Scatter(Route):
    def __init__(self, place, kind, slot, half, halves, columns, blocks, send, recv):
        super().__init__(place, kind, slot, half, send, recv)
        self.halves, self.columns, self.blocks = halves, columns, blocks

    def message(self, n):
        if n < 4:
            step = 3 if n % 2 else 1
            if n < 2:
                src, dst = self.half(self.column(2), n), self.halves(n)
            else:
                src, dst = self.column(step), self.columns(n - 2)
            return self.copy(n, src, dst, self.device(0, step))
        step = STEPS[n - 4]
        return self.copy(n, self.block(step, 0), self.blocks(n - 4), self.device(step, 0))

    def stage(self, number):
        if number == 0:
            start_all([self.message(n) for n in range(2)])
        elif number == 1:
            for n, step in ((0, 1), (1, 3)):
                self.message(n).wait_recv()
                add_into(self.half(self.column(step), n), [self.halves(n)])
                self.message(n + 2).start()
        elif number == 2:
            for n in (2, 3):
                self.message(n).wait_recv()
            for n, step in enumerate(STEPS + (0,)):
                place = (self.a + step) % 4
                add_into(self.block(step, 0), [self.columns(i).at[place] for i in range(2)])
                if step:
                    self.message(4 + n).start()
        else:
            for n in range(4, 7):
                self.message(n).wait_recv()

    def total(self):
        total = self.block(0, 0)[...].astype(F32)
        for n in range(3):
            total = total + self.blocks(n)[...].astype(F32)
        return total


class Ring(Route):
    def __init__(self, place, slot, send, recv, landing=None):
        self.place, self.slot, self.send_sems, self.recv_sems = place, slot, send, recv
        self.landing = landing

    def own(self, step):
        return self.slot((self.place.x + step) % 4)

    def drain(self):
        for n in range(3):
            self.message(n).wait_send()


class RingGather(Ring):
    def message(self, n, back=False):
        ref = self.own(4 - STEPS[n] if back else 0)
        return self.copy(n, ref, ref, self.place.along_x(STEPS[n]))

    def stage(self, number):
        if number == 0:
            start_all([self.message(n) for n in range(3)])
        else:
            for n in range(3):
                self.message(n, True).wait_recv()


class RingScatter(Ring):
    def message(self, n):
        return self.copy(n, self.own(STEPS[n]), self.landing(n), self.place.along_x(STEPS[n]))

    def stage(self, number):
        if number == 0:
            start_all([self.message(n) for n in range(3)])
        else:
            for n in range(3):
                self.message(n).wait_recv()
            add_into(self.own(0), [self.landing(n) for n in range(3)])


def tall_rows(kind, with_gain):
    return pl.ds(64, 80 if with_gain else 64) if kind else pl.ds(0, 64)


def tall_half(ref, kind, with_gain, n):
    if n == 0:
        return ref.at[:, pl.ds(0, 32)]
    return ref.at[:, pl.ds(32, 48 if kind and with_gain else 32)]


def piece_rows(number):
    return pl.ds(pl.multiple_of(number * 32, 32), 32)


def kernel(
    x_hbm, q_hbm, g_hbm, spans_ref, gain_ref, wk_hbm, wv_hbm, frequency_ref,
    out_hbm, dq_hbm, dx_hbm, dwk_ref, dwv_ref, dgain_ref,
    x_ref, q_ref, g_ref, w_first, w_rest, kvbuf, qs, gs, qt, gt, probs_low, probs_high, ds_low, ds_high,
    grads, kv_halves, kv_columns, kv_blocks, dkv, ngrad, normed, normed_t, gain_row, t_last, p_last, p_rest, q_halves, q_columns, q_blocks,
    w_halves, w_columns, w_blocks, r_land, l_land, x_send, x_gain, final, inv_ref, kpos_ref, cos_ref, sin_ref,
    io_sem, w_send, w_recv, hand_send, hand_recv, wx_send, wx_recv, kv_send, kv_recv,
    rs_send, rs_recv, pair_send, pair_recv, ws_send, ws_recv, xr_send, xr_recv, x_ssem, x_rsem,
):
    me = Place()

    def wref(h):
        return w_rest.at[h - 1] if h else w_first

    def tref(h):
        return wref(h) if h < HEADS - 1 else t_last

    def pref(h):
        return p_rest.at[h] if h < HEADS - 1 else p_last

    barrier = pltpu.get_barrier_semaphore()
    loads = [
        pltpu.make_async_copy(src, dst, io_sem.at[n])
        for n, (src, dst) in enumerate(((x_hbm, x_ref), (q_hbm, q_ref), (g_hbm, g_ref)))
    ]
    for copy in loads:
        copy.start()

    others = [device_at(me.x, me.core, (me.y + d) % 4, me.z) for d in (1, 2, 3)]
    others += [device_at(me.x, me.core, me.y, (me.z + d) % 4) for d in (1, 2, 3)]
    others += [me.along_x(d) for d in (1, 2, 3)] + [me.partner()]
    for other in others:
        pl.semaphore_signal(barrier, inc=1, device_id=other, device_id_type=MESH)

    def own_weights(h, n, source):
        if h < EARLY:
            rows, target = pl.ds(pl.multiple_of(me.core * PART, PART), PART), pl.ds(0, PART)
        else:
            rows = pl.ds(pl.multiple_of(me.core * PART + me.x * 32, 32), 32)
            target = piece_rows(me.x)
        return pltpu.make_async_copy(
            source.at[rows, pl.ds(h * HEAD, HEAD)],
            wref(h).at[me.z, me.y, me.core, target, pl.ds(n * HEAD, HEAD)],
            io_sem.at[3 + 2 * h + n],
        )

    own = [
        own_weights(h, n, source)
        for h in range(HEADS)
        for n, source in enumerate((wk_hbm, wv_hbm))
    ]
    for copy in own:
        copy.start()
    w_first[me.z, me.y, me.core, PART:BLOCK, :] = jnp.broadcast_to(
        gain_ref[...].reshape(1, SHARE), (16, SHARE)
    )
    for copy in own:
        copy.wait()
    pl.semaphore_wait(barrier, len(others))

    w_routes = [
        [
            Gather(
                me,
                kind,
                lambda z, y, h=h, kind=kind: wref(h).at[z, y, me.core, tall_rows(kind, h == 0)],
                lambda ref, n, kind=kind: tall_half(ref, kind, True, n),
                w_send.at[h, kind],
                w_recv.at[h, kind],
            )
            for kind in range(2)
        ]
        for h in range(EARLY)
    ]

    late_routes = [
        Gather(
            me,
            kind,
            lambda z, y, kind=kind: w_rest.at[
                pl.ds(EARLY - 1, HEADS - EARLY), z, y, me.core, piece_rows(me.x), pl.ds(kind * HEAD, HEAD)
            ],
            lambda ref, n: ref.at[:, :, pl.ds(16 * n, 16)],
            w_send.at[EARLY, kind],
            w_recv.at[EARLY, kind],
        )
        for kind in range(2)
    ]
    for route in late_routes:
        route.column = lambda db, route=route: w_rest.at[
            (pl.ds(EARLY - 1, HEADS - EARLY),)
            + ((slice(None), (route.b + db) % 4) if route.kind else ((route.b + db) % 4, slice(None)))
            + (me.core, piece_rows(me.x), pl.ds(route.kind * HEAD, HEAD))
        ]
    wx = {
        h: RingGather(
            me,
            lambda number, h=h: wref(h).at[:, :, me.core, piece_rows(number)],
            wx_send.at[h - EARLY],
            wx_recv.at[h - EARLY],
        )
        for h in range(EARLY, HEADS)
    }

    def hand_copy(index, ref):
        return pltpu.make_async_remote_copy(
            src_ref=ref,
            dst_ref=ref,
            send_sem=hand_send.at[index],
            recv_sem=hand_recv.at[index],
            device_id=me.partner(),
            device_id_type=MESH,
        )

    def hand_column(core, kind, db):
        b = (w_routes[0][kind].b + db) % 4
        z, y = (slice(None), b) if kind else (b, slice(None))
        return hand_copy(4 * kind + db, w_first.at[z, y, core, tall_rows(kind, True)])

    def hand_head(core, h):
        return hand_copy(7 + h, wref(h).at[:, :, core])

    def w_stage(h, number):
        for kind, route in enumerate(w_routes[h]):
            route.stage(number, lambda db, kind=kind: hand_column(me.core, kind, db).start())

    def late_stage(number):
        for route in late_routes:
            route.stage(number)

    kv_routes = [
        [
            Gather(
                me,
                kind,
                lambda z, y, h=h, kind=kind: kvbuf.at[h, kind, z, y],
                lambda ref, n: ref.at[:, n],
                kv_send.at[h, kind],
                kv_recv.at[h, kind],
            )
            for kind in range(2)
        ]
        for h in range(HEADS)
    ]

    def kv_stage(h, number):
        for route in kv_routes[h]:
            route.stage(number)

    rs_routes = [
        [
            Scatter(
                me,
                kind,
                lambda z, y, h=h, kind=kind: grads.at[h, kind, z, y],
                lambda ref, n: ref.at[:, n],
                lambda n, h=h, kind=kind: kv_halves.at[h, kind, n],
                lambda n, h=h, kind=kind: kv_columns.at[h, kind, n],
                lambda n, h=h, kind=kind: kv_blocks.at[h, kind, n],
                rs_send.at[h, kind],
                rs_recv.at[h, kind],
            )
            for kind in range(2)
        ]
        for h in range(HEADS)
    ]

    first_span = spans_ref[0, me.rank, 0]
    second_span = spans_ref[0, me.rank, 1]
    flip = first_span > second_span
    low_span = jnp.minimum(first_span, second_span)
    high_span = jnp.maximum(first_span, second_span)

    def rs_stage(h, number):
        for kind, route in enumerate(rs_routes[h]):
            route.stage(number)
            if number < 3:
                continue
            total = route.total()
            low, high = total[0], total[1]
            total = jnp.concatenate(
                [jnp.where(flip, high, low), jnp.where(flip, low, high)], axis=0
            )
            if kind == 0:
                total = total * cos_ref[...] - pltpu.roll(total, HEAD // 2, 1) * sin_ref[...]
            else:
                total = total * (1.0 / SCALE)
            dkv[h, :, kind * HEAD : (kind + 1) * HEAD] = total.astype(BF16)

    def term_rows(h):
        return pl.ds(0, BLOCK if h == HEADS - 1 else PART)

    def pair_copy(h, j):
        return pltpu.make_async_remote_copy(
            src_ref=tref(h).at[j, :, 1 - me.core, term_rows(h)],
            dst_ref=pref(h).at[j],
            send_sem=pair_send.at[h, j],
            recv_sem=pair_recv.at[h, j],
            device_id=me.partner(),
            device_id_type=MESH,
        )

    def pair_sum(h):
        def group(j, carry):
            pair_copy(h, j).wait_recv()

            add_into(tref(h).at[j, :, me.core, term_rows(h)], [pref(h).at[j]])
            return carry

        lax.fori_loop(0, 4, group, 0)

    xr_routes = [
        RingScatter(
            me,
            lambda number, h=h: tref(h).at[:, :, me.core, piece_rows(number)],
            xr_send.at[h],
            xr_recv.at[h],
            lambda n, h=h: r_land.at[h, n],
        )
        for h in range(HEADS - 1)
    ]
    xr_routes.append(
        RingScatter(
            me,
            lambda number: x_send.at[piece_rows(number)],
            xr_send.at[HEADS - 1],
            xr_recv.at[HEADS - 1],
            lambda n: l_land.at[n],
        )
    )
    ws_routes = [
        [
            Scatter(
                me,
                kind,
                lambda z, y, h=h, kind=kind: tref(h).at[
                    z, y, me.core, piece_rows(me.x), pl.ds(kind * HEAD, HEAD)
                ],
                lambda ref, n: ref.at[:, pl.ds(16 * n, 16)],
                lambda n, h=h, kind=kind: q_halves.at[h, kind, n],
                lambda n, h=h, kind=kind: q_columns.at[h, kind, n],
                lambda n, h=h, kind=kind: q_blocks.at[h, kind, n],
                ws_send.at[h, kind],
                ws_recv.at[h, kind],
            )
            for kind in range(2)
        ]
        for h in range(HEADS - 1)
    ]
    ws_routes.append(
        [
            Scatter(
                me,
                kind,
                lambda z, y, kind=kind: t_last.at[z, y, me.core, tall_rows(kind, True)],
                lambda ref, n, kind=kind: tall_half(ref, kind, True, n),
                lambda n, kind=kind: w_halves.at[kind, n, :, pl.ds(0, 48 if kind and n else 32)],
                lambda n, kind=kind: w_columns.at[kind, n, :, pl.ds(0, 80 if kind else 64)],
                lambda n, kind=kind: w_blocks.at[kind, n, pl.ds(0, 80 if kind else 64)],
                ws_send.at[HEADS - 1, kind],
                ws_recv.at[HEADS - 1, kind],
            )
            for kind in range(2)
        ]
    )

    def xr_stage(h, number):
        xr_routes[h].stage(number)

    def ws_stage(h, number):
        for kind, route in enumerate(ws_routes[h]):
            route.stage(number)
            if number < 3:
                continue
            total = route.total().astype(BF16)
            if h < HEADS - 1:
                final[
                    me.core, h, piece_rows(me.x), kind * HEAD : (kind + 1) * HEAD
                ] = total
            else:
                x_send[64 * kind : 64 * kind + (80 if kind else 64), :] = total

    def columns_of(j):
        return pl.ds(pl.multiple_of(((j % 2) * 2 + j // 2) * FOUR, FOUR), FOUR)

    def unit_piece(j):
        return x_ref[:, columns_of(j)].astype(F32) * inv_ref[...]

    def weight_block(h, j):
        return wref(h)[j, :, :, 0:PART, :].reshape(FOUR, 2 * HEAD)

    def positions():
        row = lax.broadcasted_iota(jnp.int32, (ROWS, 1), 0)
        place = jnp.where(row < SPAN, first_span * SPAN + row, second_span * SPAN + row - SPAN)
        angle = place.astype(F32) * frequency_ref[...]
        lane = lax.broadcasted_iota(jnp.int32, (ROWS, HEAD), 1)
        sine = jnp.sin(angle)
        cos_ref[...] = jnp.cos(angle)
        sin_ref[...] = jnp.where(lane < HEAD // 2, -sine, sine)
        lane = lax.broadcasted_iota(jnp.int32, (1, HEAD), 1)
        for s in range(0, RANKS, 2):
            ranks = [rank_at((s + n) % 4, (s + n) // 4) for n in range(2)]
            pairs = [(spans_ref[0, r, 0], spans_ref[0, r, 1]) for r in ranks]
            for half, pick in ((0, jnp.minimum), (1, jnp.maximum)):
                left, right = pick(*pairs[0]), pick(*pairs[1])
                kpos_ref[half : half + 1, s * SPAN : s * SPAN + HEAD] = jnp.where(
                    lane < SPAN, left * SPAN + lane, right * SPAN + lane - SPAN
                )

    def normalise():
        squares = jnp.zeros((ROWS, HEAD), F32)
        for c in range(FEATURES // HEAD):
            piece = x_ref[:, c * HEAD : (c + 1) * HEAD].astype(F32)
            squares = squares + piece * piece
        inv_ref[...] = lax.rsqrt(
            jnp.sum(squares, axis=-1, keepdims=True) * (1.0 / FEATURES) + EPSILON
        )

    def prepare():
        for j in range(4):
            for y in range(4):
                gain_row[j, :, y * SHARE : (y + 1) * SHARE] = w_first[
                    j, y, 0, PART:BLOCK, :
                ].astype(F32)[0:1, :]
            normed[j] = (unit_piece(j) * gain_row[j]).astype(BF16)

    def turn():
        for j in range(4):
            normed_t[j] = jnp.transpose(normed[j].astype(F32)).astype(BF16)

    def project(h):
        raw = dot(normed[0], weight_block(h, 0))
        for j in range(1, 4):
            raw = raw + dot(normed[j], weight_block(h, j))
        key = raw[:, 0:HEAD]
        key = key * cos_ref[...] + pltpu.roll(key, HEAD // 2, 1) * sin_ref[...]
        for kind, array in ((0, key), (1, raw[:, HEAD:])):
            kvbuf[h, kind, me.z, me.y, 0] = jnp.where(flip, array[SPAN:], array[:SPAN]).astype(BF16)
            kvbuf[h, kind, me.z, me.y, 1] = jnp.where(flip, array[:SPAN], array[SPAN:]).astype(BF16)

    def weight_terms(h):
        last = h == HEADS - 1

        def group(j, mean):
            grad = dkv[h]
            back = dot_nt(grad, weight_block(h, j))
            block = dot(normed_t[j], grad).astype(BF16)
            tref(h)[j, :, :, 0:PART, :] = block.reshape(4, 2, PART, 2 * HEAD)
            if h:
                back = back + ngrad[j]
            if last:
                unit = unit_piece(j)
                gain = jnp.sum(unit * back, axis=0, keepdims=True)
                for y in range(4):
                    piece = jnp.broadcast_to(gain[:, y * SHARE : (y + 1) * SHARE], (16, SHARE))
                    for part in range(2):
                        t_last[j, y, part, PART:BLOCK, :] = piece.astype(BF16)
                back = back * gain_row[j]
                mean = mean + jnp.sum(back * unit, axis=-1, keepdims=True)
            ngrad[j] = back
            pair_copy(h, j).start()
            return mean

        return lax.fori_loop(0, 4, group, jnp.zeros((ROWS, 1), F32))

    token = lax.broadcasted_iota(jnp.int32, (WIDTH, 1), 0) % SPAN
    q_pos = (low_span * SPAN + token, high_span * SPAN + token)

    def load_head(h):
        for n in range(GROUP):
            column = pl.ds(pl.multiple_of((h * GROUP + n) * HEAD, HEAD), HEAD)
            for source, target in ((q_ref, qs), (g_ref, gs)):
                first, second = source[0:SPAN, column], source[SPAN:ROWS, column]
                target[0, n * SPAN : (n + 1) * SPAN, :] = jnp.where(flip, second, first)
                target[1, n * SPAN : (n + 1) * SPAN, :] = jnp.where(flip, first, second)

    def store_head(h):
        for n in range(GROUP):
            column = pl.ds(pl.multiple_of((h * GROUP + n) * HEAD, HEAD), HEAD)
            for source, target in ((qs, q_ref), (gs, g_ref)):
                low = source[0, n * SPAN : (n + 1) * SPAN, :]
                high = source[1, n * SPAN : (n + 1) * SPAN, :]
                target[0:SPAN, column] = jnp.where(flip, high, low)
                target[SPAN:ROWS, column] = jnp.where(flip, low, high)

    def attend(h, half):
        def block(kind, side):
            return kvbuf[h, kind, :, :, side].reshape(RANKS * SPAN, HEAD)

        place_rows = slice(half * WIDTH, (half + 1) * WIDTH)
        q, g = qs[half], gs[half]
        scores = [dot_nt(q, block(0, k)) for k in range(half + 1)]
        scores[half] = jnp.where(
            kpos_ref[half : half + 1, :] <= q_pos[half], scores[half], NEG_FILL
        )
        top = jnp.max(scores[0], axis=-1, keepdims=True)
        if half:
            top = jnp.maximum(top, jnp.max(scores[1], axis=-1, keepdims=True))
        weights = [jnp.exp2((s - top) * EXP_SCALE) for s in scores]
        total = jnp.sum(weights[0], axis=-1, keepdims=True)
        if half:
            total = total + jnp.sum(weights[1], axis=-1, keepdims=True)
        low = [w.astype(BF16) for w in weights]
        attended = dot(low[0], block(1, 0))
        if half:
            attended = attended + dot(low[1], block(1, 1))
        share = 1.0 / total
        attended = (attended * share).astype(BF16)
        grad = (g.astype(F32) * (share * SCALE)).astype(BF16)
        grad_f = grad.astype(F32)
        row_dot = jnp.sum(grad_f * attended.astype(F32), axis=-1, keepdims=True)
        gt[:, place_rows] = jnp.transpose(grad_f).astype(BF16)
        qt[:, place_rows] = jnp.transpose(q.astype(F32)).astype(BF16)
        back = None
        for k in range(half + 1):
            dots = dot_nt(grad, block(1, k))
            ds = (low[k].astype(F32) * (dots - row_dot)).astype(BF16)
            if k:
                probs_high[...] = low[k]
                ds_high[...] = ds
            else:
                probs_low[place_rows, :] = low[k]
                ds_low[place_rows, :] = ds
            term = dot(ds, block(0, k))
            back = term if back is None else back + term
        qs[half] = back.astype(BF16)
        gs[half] = attended

    def key_terms(h):
        for kind, left, low, high in ((0, qt, ds_low, ds_high), (1, gt, probs_low, probs_high)):
            for side, array in (
                (0, dot(left[...], low[...])),
                (1, dot(left[:, WIDTH:], high[...])),
            ):
                grads[h, kind, :, :, side] = (
                    jnp.transpose(array).astype(BF16).reshape(4, 4, SPAN, HEAD)
                )

    def late_arrival(h):
        wx[h].stage(1)
        hand_head(me.core, h).start()

    def late_projection(h):
        hand_head(1 - me.core, h).wait_recv()
        project(h)
        kv_stage(h, 0)

    late_stage(0)
    w_stage(0, 0)
    positions()
    loads[0].wait()
    normalise()
    late_stage(1)
    w_stage(0, 1)
    late_stage(2)
    w_stage(0, 2)
    late_stage(3)
    for h in range(EARLY, HEADS):
        wx[h].stage(0)
    w_stage(0, 3)
    for kind in range(2):
        for db in range(4):
            hand_column(1 - me.core, kind, db).wait_recv()
    prepare()
    project(0)
    kv_stage(0, 0)
    turn()
    kv_stage(0, 1)
    late_arrival(1)
    kv_stage(0, 2)
    late_projection(1)
    loads[1].wait()
    loads[2].wait()
    load_head(0)
    kv_stage(0, 3)

    def xr_begin(h):
        pair_sum(h)
        xr_stage(h, 0)

    def xr_end(h):
        xr_stage(h, 1)
        ws_stage(h, 0)

    def weights_left():
        for routes in w_routes + [late_routes]:
            for route in routes:
                route.drain()
        for route in wx.values():
            route.drain()
        for kind in range(2):
            for db in range(4):
                hand_column(me.core, kind, db).wait_send()
        for h in range(1, HEADS):
            hand_head(me.core, h).wait_send()

    plan = {
        (0, 0): [lambda: kv_stage(1, 1), lambda: late_arrival(2)],
        (0, 1): [lambda: late_projection(2)],
        (0, 2): [lambda: kv_stage(1, 2), lambda: kv_stage(2, 1), lambda: late_arrival(3)],
        (0, 3): [lambda: rs_stage(0, 0)],
        (0, 4): [lambda: late_projection(3), lambda: kv_stage(1, 3)],
        (1, 1): [lambda: kv_stage(2, 2), lambda: rs_stage(0, 1)],
        (1, 2): [lambda: kv_stage(3, 1), lambda: rs_stage(0, 2)],
        (1, 3): [lambda: rs_stage(1, 0)],
        (1, 4): [weights_left, lambda: kv_stage(2, 3), lambda: kv_stage(3, 2)],
        (2, 1): [lambda: rs_stage(0, 3), lambda: weight_terms(0), lambda: rs_stage(1, 1)],
        (2, 2): [lambda: xr_begin(0), lambda: rs_stage(1, 2)],
        (2, 3): [lambda: rs_stage(2, 0)],
        (2, 4): [lambda: rs_stage(1, 3), lambda: weight_terms(1), lambda: kv_stage(3, 3)],
        (3, 1): [lambda: rs_stage(2, 1), lambda: xr_begin(1)],
        (3, 2): [lambda: rs_stage(2, 2), lambda: xr_end(0)],
        (3, 3): [lambda: rs_stage(3, 0), lambda: ws_stage(0, 1)],
        (3, 4): [lambda: rs_stage(2, 3), lambda: weight_terms(2)],
    }

    def one_head(h, carry):
        def serve(point):
            for head in range(HEADS):
                if (head, point) not in plan:
                    continue

                @pl.when(h == head)
                def _():
                    for item in plan[head, point]:
                        item()

        serve(0)
        attend(h, 0)
        serve(1)
        attend(h, 1)
        serve(2)
        key_terms(h)
        serve(3)
        store_head(h)

        @pl.when(h < HEADS - 1)
        def _():
            load_head(h + 1)

        serve(4)
        return carry

    lax.fori_loop(0, HEADS, one_head, 0)

    stores = [
        pltpu.make_async_copy(g_ref, out_hbm, io_sem.at[0]),
        pltpu.make_async_copy(q_ref, dq_hbm, io_sem.at[1]),
    ]
    for copy in stores:
        copy.start()

    def x_copy(index, ref, dst, to):
        return pltpu.make_async_remote_copy(
            src_ref=ref,
            dst_ref=dst,
            send_sem=x_ssem.at[index],
            recv_sem=x_rsem.at[index],
            device_id=to,
            device_id_type=MESH,
        )

    def spread(base, heads, d, owner):
        ref = final.at[me.core, heads, piece_rows(owner)]
        return x_copy(base + d - 1, ref, ref, me.along_x(d))

    def to_partner(index, heads, core):
        ref = final.at[core, heads]
        return x_copy(index, ref, ref, me.partner())

    def spread_start(base, heads):
        for d in (1, 2, 3):
            spread(base, heads, d, me.x).start()

    def spread_wait(base, heads):
        for d in (1, 2, 3):
            spread(base, heads, d, (me.x + 4 - d) % 4).wait_recv()

    early_heads, late_head = pl.ds(0, HEADS - 1), pl.ds(HEADS - 1, 1)
    rs_stage(3, 1)
    xr_begin(2)
    ws_stage(0, 2)
    rs_stage(3, 2)
    xr_end(1)
    ws_stage(0, 3)
    rs_stage(3, 3)
    mean = weight_terms(3) * (1.0 / FEATURES)
    pair_sum(3)
    ws_stage(3, 0)
    ws_stage(1, 1)

    def row_grad(j, carry):
        dx = inv_ref[...] * (ngrad[j] - unit_piece(j) * mean)
        x_ref[:, columns_of(j)] = dx.astype(BF16)
        return carry

    lax.fori_loop(0, 4, row_grad, 0)
    stores.append(pltpu.make_async_copy(x_ref, dx_hbm, io_sem.at[2]))
    stores[2].start()
    ws_stage(3, 1)
    ws_stage(1, 2)
    xr_end(2)
    ws_stage(3, 2)
    ws_stage(1, 3)
    ws_stage(2, 1)
    ws_stage(3, 3)
    xr_stage(3, 0)
    gains = [
        x_copy(5 + d, x_send.at[pl.ds(PART, 16)], x_gain.at[d - 1], me.along_x(d))
        for d in (1, 2, 3)
    ]
    for copy in gains:
        copy.start()
    ws_stage(2, 2)
    xr_stage(3, 1)
    final[me.core, HEADS - 1, piece_rows(me.x)] = x_send[piece_rows(me.x), :]
    spread_start(3, late_head)
    ws_stage(2, 3)
    spread_start(0, early_heads)
    spread_wait(0, early_heads)
    to_partner(9, early_heads, me.core).start()
    for copy in gains:
        copy.wait_recv()
    total = x_send[PART:BLOCK, :].astype(F32)
    for d in range(3):
        total = total + x_gain[d].astype(F32)
    dgain_ref[...] = total[0:8, :]
    spread_wait(3, late_head)
    to_partner(10, late_head, me.core).start()

    def write_weights(heads):
        for h in heads:
            for core in range(2):
                rows, columns = slice(core * PART, (core + 1) * PART), slice(h * HEAD, (h + 1) * HEAD)
                dwk_ref[rows, columns] = final[core, h, :, 0:HEAD].astype(F32)
                dwv_ref[rows, columns] = final[core, h, :, HEAD:].astype(F32)

    to_partner(9, early_heads, 1 - me.core).wait_recv()
    write_weights(range(HEADS - 1))
    to_partner(10, late_head, 1 - me.core).wait_recv()
    write_weights((HEADS - 1,))

    for routes in kv_routes + rs_routes + ws_routes:
        for route in routes:
            route.drain()
    for route in xr_routes:
        route.drain()
    for h in range(HEADS):
        for j in range(4):
            pair_copy(h, j).wait_send()
    for copy in gains:
        copy.wait_send()
    for base, heads in ((0, early_heads), (3, late_head)):
        for d in (1, 2, 3):
            spread(base, heads, d, me.x).wait_send()
    to_partner(9, early_heads, me.core).wait_send()
    to_partner(10, late_head, me.core).wait_send()
    for copy in stores:
        copy.wait()


def settle(*refs):
    for n in range(5):
        refs[6 + n][...] = refs[n][...]
    refs[11][...] = refs[5][0, :]


def local(inputs, queries, out_grad, span_ids, norm_gain, key_weight, value_weight):
    frequency = np.exp(
        -math.log(ROPE_BASE) * (2.0 * np.arange(HEAD // 2, dtype=np.float32) / HEAD)
    ).astype(np.float32)
    frequency = jnp.asarray(np.concatenate([frequency, frequency])[None, :])
    anywhere = pl.BlockSpec(memory_space=pl.ANY)
    vmem = pl.BlockSpec(memory_space=pltpu.VMEM)
    smem = pl.BlockSpec(memory_space=pltpu.SMEM)
    dma = pltpu.SemaphoreType.DMA
    outs = pl.pallas_call(
        kernel,
        out_shape=[
            jax.ShapeDtypeStruct((ROWS, FEATURES), BF16),
            jax.ShapeDtypeStruct((ROWS, FEATURES), BF16),
            jax.ShapeDtypeStruct((ROWS, FEATURES), BF16),
            jax.ShapeDtypeStruct((SHARE, WIDTH), F32),
            jax.ShapeDtypeStruct((SHARE, WIDTH), F32),
            jax.ShapeDtypeStruct((8, SHARE), F32),
        ],
        in_specs=[anywhere] * 3 + [smem, vmem] + [anywhere] * 2 + [vmem],
        out_specs=[anywhere] * 3 + [vmem] * 3,
        scratch_shapes=[
            pltpu.VMEM((ROWS, FEATURES), BF16),
            pltpu.VMEM((ROWS, FEATURES), BF16),
            pltpu.VMEM((ROWS, FEATURES), BF16),
            pltpu.VMEM((4, 4, 2, BLOCK, 2 * HEAD), BF16),
            pltpu.VMEM((HEADS - 1, 4, 4, 2, PART, 2 * HEAD), BF16),
            pltpu.VMEM((HEADS, 2, 4, 4, 2, SPAN, HEAD), BF16),
            pltpu.VMEM((2, WIDTH, HEAD), BF16),
            pltpu.VMEM((2, WIDTH, HEAD), BF16),
            pltpu.VMEM((HEAD, 2 * WIDTH), BF16),
            pltpu.VMEM((HEAD, 2 * WIDTH), BF16),
            pltpu.VMEM((2 * WIDTH, RANKS * SPAN), BF16),
            pltpu.VMEM((WIDTH, RANKS * SPAN), BF16),
            pltpu.VMEM((2 * WIDTH, RANKS * SPAN), BF16),
            pltpu.VMEM((WIDTH, RANKS * SPAN), BF16),
            pltpu.VMEM((HEADS, 2, 4, 4, 2, SPAN, HEAD), BF16),
            pltpu.VMEM((HEADS, 2, 2, 4, SPAN, HEAD), BF16),
            pltpu.VMEM((HEADS, 2, 2, 4, 2, SPAN, HEAD), BF16),
            pltpu.VMEM((HEADS, 2, 3, 2, SPAN, HEAD), BF16),
            pltpu.VMEM((HEADS, ROWS, 2 * HEAD), BF16),
            pltpu.VMEM((4, ROWS, FOUR), F32),
            pltpu.VMEM((4, ROWS, FOUR), BF16),
            pltpu.VMEM((4, FOUR, ROWS), BF16),
            pltpu.VMEM((4, 1, FOUR), F32),
            pltpu.VMEM((4, 4, 2, BLOCK, 2 * HEAD), BF16),
            pltpu.VMEM((4, 4, BLOCK, 2 * HEAD), BF16),
            pltpu.VMEM((HEADS - 1, 4, 4, PART, 2 * HEAD), BF16),
            pltpu.VMEM((HEADS - 1, 2, 2, 4, 16, HEAD), BF16),
            pltpu.VMEM((HEADS - 1, 2, 2, 4, 32, HEAD), BF16),
            pltpu.VMEM((HEADS - 1, 2, 3, 32, HEAD), BF16),
            pltpu.VMEM((2, 2, 4, 48, 2 * HEAD), BF16),
            pltpu.VMEM((2, 2, 4, 80, 2 * HEAD), BF16),
            pltpu.VMEM((2, 3, 80, 2 * HEAD), BF16),
            pltpu.VMEM((HEADS - 1, 3, 4, 4, 32, 2 * HEAD), BF16),
            pltpu.VMEM((3, 32, 2 * HEAD), BF16),
            pltpu.VMEM((BLOCK, 2 * HEAD), BF16),
            pltpu.VMEM((3, 16, 2 * HEAD), BF16),
            pltpu.VMEM((2, HEADS, PART, 2 * HEAD), BF16),
            pltpu.VMEM((ROWS, 1), F32),
            pltpu.VMEM((2, RANKS * SPAN), jnp.int32),
            pltpu.VMEM((ROWS, HEAD), F32),
            pltpu.VMEM((ROWS, HEAD), F32),
            dma((3 + 2 * HEADS,)),
            dma((EARLY + 1, 2, 7)), dma((EARLY + 1, 2, 7)),
            dma((7 + HEADS,)), dma((7 + HEADS,)),
            dma((HEADS - EARLY, 3)), dma((HEADS - EARLY, 3)),
            dma((HEADS, 2, 7)), dma((HEADS, 2, 7)),
            dma((HEADS, 2, 7)), dma((HEADS, 2, 7)),
            dma((HEADS, 4)), dma((HEADS, 4)),
            dma((HEADS, 2, 7)), dma((HEADS, 2, 7)),
            dma((HEADS, 3)), dma((HEADS, 3)),
            dma((11,)), dma((11,)),
        ],
        compiler_params=pltpu.CompilerParams(
            collective_id=0, has_side_effects=True, vmem_limit_bytes=55 * 1024 * 1024
        ),
        cost_estimate=pl.CostEstimate(
            flops=12 * 10**9, bytes_accessed=10**7, transcendentals=7 * 10**6
        ),
        name="layer",
    )(
        inputs, queries, out_grad, span_ids, norm_gain, key_weight, value_weight, frequency
    )
    blocks = [pl.BlockSpec((ROWS, FEATURES // 4), lambda i: (0, i))] * 3
    blocks += [pl.BlockSpec((SHARE // 4, WIDTH), lambda i: (i, 0))] * 2
    gains = [pl.BlockSpec((8, SHARE), lambda i: (0, 0)), pl.BlockSpec((SHARE,), lambda i: (0,))]
    outs = pl.pallas_call(
        settle,
        out_shape=[jax.ShapeDtypeStruct(o.shape, o.dtype) for o in outs[:5]]
        + [jax.ShapeDtypeStruct((SHARE,), F32)],
        grid=(4,),
        in_specs=blocks + gains[:1],
        out_specs=blocks + gains[1:],
        name="settle",
    )(*outs)
    return tuple(outs)


def solution(mesh):
    tokens = P(("dp", "shard", "ctx"), None)
    rows = P(("shard", "ctx"), None)
    return jax.shard_map(
        local,
        mesh=mesh,
        in_specs=(tokens, tokens, tokens, P("dp", None, None), P(("shard", "ctx")), rows, rows),
        out_specs=(tokens, tokens, tokens, rows, rows, P(("shard", "ctx"))),
        check_vma=False,
    )
```

```python
import functools
import math

import jax
import jax.numpy as jnp
import numpy as np
from jax import lax
from jax.experimental import pallas as pl
from jax.experimental.pallas import tpu as pltpu
from jax.sharding import PartitionSpec as P

HEAD = 128
HEADS = 4
GROUP = 8
SPAN = 64
RANKS = 16
ROWS = 128
FEATURES = 4096
SHARE = 256
WIDTH = 512
BLOCK = 144
FOUR = 1024
PART = 128
EARLY = 1
EPSILON = 1e-05
ROPE_BASE = 500000.0
NEG_FILL = -1e30
SCALE = HEAD ** (-0.5)
EXP_SCALE = SCALE * math.log2(math.e)
MESH = pl.DeviceIdType.MESH
F32 = jnp.float32
BF16 = jnp.bfloat16
NT = (((1,), (1,)), ((), ()))


def device_at(x, core, y, z):
    return (x * 2 + core, z % 2, (z // 2) * 4 + y)


def rank_at(y, z):
    return (z % 2) * 8 + (z // 2) * 4 + y


def dot(a, b):
    return jnp.dot(a, b, preferred_element_type=F32)


def dot_nt(a, b):
    return lax.dot_general(a, b, NT, preferred_element_type=F32)


class Place:
    def __init__(self):
        dp = lax.axis_index("dp")
        shard = lax.axis_index("shard")
        ctx = lax.axis_index("ctx")
        self.x = dp // 2
        self.core = dp % 2
        self.y = ctx % 4
        self.z = (ctx // 4) * 2 + shard
        self.rank = rank_at(self.y, self.z)

    def partner(self):
        return device_at(self.x, 1 - self.core, self.y, self.z)

    def along_x(self, step):
        return device_at((self.x + step) % 4, self.core, self.y, self.z)


STEPS = (1, 3, 2)


def start_all(copies):
    for copy in copies:
        copy.start()


def add_into(ref, others):
    total = ref[...].astype(F32)
    for other in others:
        total = total + other[...].astype(F32)
    ref[...] = total.astype(BF16)


class Route:
    direct = False

    def __init__(self, place, kind, slot, half, send, recv):
        self.place, self.kind, self.slot, self.half = place, kind, slot, half
        self.send_sems, self.recv_sems = send, recv
        self.a, self.b = (place.z, place.y) if kind else (place.y, place.z)

    def block(self, da, db):
        a, b = (self.a + da) % 4, (self.b + db) % 4
        return self.slot(a, b) if self.kind else self.slot(b, a)

    def column(self, db):
        b = (self.b + db) % 4
        return self.slot(slice(None), b) if self.kind else self.slot(b, slice(None))

    def device(self, da, db):
        a, b = (self.a + da) % 4, (self.b + db) % 4
        y, z = (b, a) if self.kind else (a, b)
        return device_at(self.place.x, self.place.core, y, z)

    def copy(self, index, src, dst, to):
        return pltpu.make_async_remote_copy(
            src_ref=src,
            dst_ref=dst,
            send_sem=self.send_sems.at[index],
            recv_sem=self.recv_sems.at[index],
            device_id=to,
            device_id_type=MESH,
        )

    def drain(self):
        for n in self.direct_copies if self.direct else range(7):
            self.message(n).wait_send()


class Gather(Route):
    direct_copies = range(6)

    def message(self, n, back=False):
        if n < 3:
            ref = self.block(4 - STEPS[n] if back else 0, 0)
            return self.copy(n, ref, ref, self.device(STEPS[n], 0))
        if self.direct:
            step = STEPS[n - 3]
            ref = self.column(4 - step if back else 0)
            return self.copy(n, ref, ref, self.device(0, step))
        step = 1 if n % 2 else 3
        if n < 5:
            ref = self.column(4 - step if back else 0)
        else:
            ref = self.half(self.column(2 if back else 4 - step), n - 5)
        return self.copy(n, ref, ref, self.device(0, step))

    def stage(self, number, arrived=lambda db: None):
        if number == 0:
            start_all([self.message(n) for n in range(3)])
        elif number == 1:
            for n in range(3):
                self.message(n, True).wait_recv()
            start_all([self.message(n) for n in ((3, 4, 5) if self.direct else (3, 4))])
            arrived(0)
        elif self.direct:
            for n in (3, 4, 5) if number == 2 else ():
                self.message(n, True).wait_recv()
                arrived(4 - STEPS[n - 3])
        elif number == 2:
            for n, db in ((3, 3), (4, 1)):
                self.message(n, True).wait_recv()
                self.message(n + 2).start()
                arrived(db)
        else:
            for n in (5, 6):
                self.message(n, True).wait_recv()
            arrived(2)


class Scatter(Route):
    direct_copies = (0, 1, 2, 4, 5, 6)

    def __init__(self, place, kind, slot, half, halves, columns, blocks, send, recv):
        super().__init__(place, kind, slot, half, send, recv)
        self.halves, self.columns, self.blocks = halves, columns, blocks

    def message(self, n):
        if n < 3 and self.direct:
            step = STEPS[n]
            return self.copy(n, self.column(step), self.columns(n), self.device(0, step))
        if n < 4:
            step = 3 if n % 2 else 1
            if n < 2:
                src, dst = self.half(self.column(2), n), self.halves(n)
            else:
                src, dst = self.column(step), self.columns(n - 2)
            return self.copy(n, src, dst, self.device(0, step))
        step = STEPS[n - 4]
        return self.copy(n, self.block(step, 0), self.blocks(n - 4), self.device(step, 0))

    def stage(self, number):
        if number == 0:
            start_all([self.message(n) for n in range(3 if self.direct else 2)])
        elif number == 1:
            for n, step in () if self.direct else ((0, 1), (1, 3)):
                self.message(n).wait_recv()
                add_into(self.half(self.column(step), n), [self.halves(n)])
                self.message(n + 2).start()
        elif number == 2:
            for n in (0, 1, 2) if self.direct else (2, 3):
                self.message(n).wait_recv()
            for n, step in enumerate(STEPS + (0,)):
                place = (self.a + step) % 4
                add_into(
                    self.block(step, 0),
                    [self.columns(i).at[place] for i in range(3 if self.direct else 2)],
                )
                if step:
                    self.message(4 + n).start()
        else:
            for n in range(4, 7):
                self.message(n).wait_recv()

    def total(self):
        total = self.block(0, 0)[...].astype(F32)
        for n in range(3):
            total = total + self.blocks(n)[...].astype(F32)
        return total


class Ring(Route):
    def __init__(self, place, slot, send, recv, landing=None):
        self.place, self.slot, self.send_sems, self.recv_sems = place, slot, send, recv
        self.landing = landing

    def own(self, step):
        return self.slot((self.place.x + step) % 4)

    def drain(self):
        for n in range(3):
            self.message(n).wait_send()


class RingGather(Ring):
    def message(self, n, back=False):
        ref = self.own(4 - STEPS[n] if back else 0)
        return self.copy(n, ref, ref, self.place.along_x(STEPS[n]))

    def stage(self, number):
        if number == 0:
            start_all([self.message(n) for n in range(3)])
        else:
            for n in range(3):
                self.message(n, True).wait_recv()


class RingScatter(Ring):
    def message(self, n):
        return self.copy(n, self.own(STEPS[n]), self.landing(n), self.place.along_x(STEPS[n]))

    def stage(self, number):
        if number == 0:
            start_all([self.message(n) for n in range(3)])
        else:
            for n in range(3):
                self.message(n).wait_recv()
            add_into(self.own(0), [self.landing(n) for n in range(3)])


def tall_rows(kind, with_gain):
    return pl.ds(64, 80 if with_gain else 64) if kind else pl.ds(0, 64)


def tall_half(ref, kind, with_gain, n):
    if n == 0:
        return ref.at[:, pl.ds(0, 32)]
    return ref.at[:, pl.ds(32, 48 if kind and with_gain else 32)]


def piece_rows(number):
    return pl.ds(pl.multiple_of(number * 32, 32), 32)


def kernel(
    x_hbm, q_hbm, g_hbm, spans_ref, gain_ref, wk_hbm, wv_hbm, frequency_ref,
    out_hbm, dq_hbm, dx_hbm, dwk_ref, dwv_ref, dgain_ref,
    x_ref, q_ref, g_ref, w_first, w_rest, kvbuf, qs, gs, qt, gt, probs_low, probs_high, ds_low, ds_high,
    grads, kv_halves, kv_columns, kv_third, kv_blocks, dkv, ngrad, normed, normed_t, gain_row, t_last, p_last, p_rest, q_halves, q_columns, q_blocks,
    w_halves, w_columns, w_third, w_blocks, r_land, l_land, x_send, x_gain, final, inv_ref, kpos_ref, cos_ref, sin_ref,
    io_sem, w_send, w_recv, hand_send, hand_recv, wx_send, wx_recv, kv_send, kv_recv,
    rs_send, rs_recv, pair_send, pair_recv, ws_send, ws_recv, xr_send, xr_recv, x_ssem, x_rsem,
):
    me = Place()

    def wref(h):
        return w_rest.at[h - 1] if h else w_first

    def tref(h):
        return wref(h) if h < HEADS - 1 else t_last

    def pref(h):
        return p_rest.at[h] if h < HEADS - 1 else p_last

    barrier = pltpu.get_barrier_semaphore()
    loads = [
        pltpu.make_async_copy(src, dst, io_sem.at[n])
        for n, (src, dst) in enumerate(((x_hbm, x_ref), (q_hbm, q_ref), (g_hbm, g_ref)))
    ]
    for copy in loads:
        copy.start()

    others = [device_at(me.x, me.core, (me.y + d) % 4, me.z) for d in (1, 2, 3)]
    others += [device_at(me.x, me.core, me.y, (me.z + d) % 4) for d in (1, 2, 3)]
    others += [me.along_x(d) for d in (1, 2, 3)] + [me.partner()]
    for other in others:
        pl.semaphore_signal(barrier, inc=1, device_id=other, device_id_type=MESH)

    def own_weights(h, n, source):
        if h < EARLY:
            rows, target = pl.ds(pl.multiple_of(me.core * PART, PART), PART), pl.ds(0, PART)
        else:
            rows = pl.ds(pl.multiple_of(me.core * PART + me.x * 32, 32), 32)
            target = piece_rows(me.x)
        return pltpu.make_async_copy(
            source.at[rows, pl.ds(h * HEAD, HEAD)],
            wref(h).at[me.z, me.y, me.core, target, pl.ds(n * HEAD, HEAD)],
            io_sem.at[3 + 2 * h + n],
        )

    own = [
        own_weights(h, n, source)
        for h in range(HEADS)
        for n, source in enumerate((wk_hbm, wv_hbm))
    ]
    for copy in own:
        copy.start()
    w_first[me.z, me.y, me.core, PART:BLOCK, :] = jnp.broadcast_to(
        gain_ref[...].reshape(1, SHARE), (16, SHARE)
    )
    for copy in own:
        copy.wait()
    pl.semaphore_wait(barrier, len(others))

    w_routes = [
        [
            Gather(
                me,
                kind,
                lambda z, y, h=h, kind=kind: wref(h).at[z, y, me.core, tall_rows(kind, h == 0)],
                lambda ref, n, kind=kind: tall_half(ref, kind, True, n),
                w_send.at[h, kind],
                w_recv.at[h, kind],
            )
            for kind in range(2)
        ]
        for h in range(EARLY)
    ]

    late_routes = [
        Gather(
            me,
            kind,
            lambda z, y, kind=kind: w_rest.at[
                pl.ds(EARLY - 1, HEADS - EARLY), z, y, me.core, piece_rows(me.x), pl.ds(kind * HEAD, HEAD)
            ],
            lambda ref, n: ref.at[:, :, pl.ds(16 * n, 16)],
            w_send.at[EARLY, kind],
            w_recv.at[EARLY, kind],
        )
        for kind in range(2)
    ]
    for route in late_routes:
        route.column = lambda db, route=route: w_rest.at[
            (pl.ds(EARLY - 1, HEADS - EARLY),)
            + ((slice(None), (route.b + db) % 4) if route.kind else ((route.b + db) % 4, slice(None)))
            + (me.core, piece_rows(me.x), pl.ds(route.kind * HEAD, HEAD))
        ]
    wx = {
        h: RingGather(
            me,
            lambda number, h=h: wref(h).at[:, :, me.core, piece_rows(number)],
            wx_send.at[h - EARLY],
            wx_recv.at[h - EARLY],
        )
        for h in range(EARLY, HEADS)
    }

    def hand_copy(index, ref):
        return pltpu.make_async_remote_copy(
            src_ref=ref,
            dst_ref=ref,
            send_sem=hand_send.at[index],
            recv_sem=hand_recv.at[index],
            device_id=me.partner(),
            device_id_type=MESH,
        )

    def hand_column(core, kind, db):
        b = (w_routes[0][kind].b + db) % 4
        z, y = (slice(None), b) if kind else (b, slice(None))
        return hand_copy(4 * kind + db, w_first.at[z, y, core, tall_rows(kind, True)])

    def hand_head(core, h):
        return hand_copy(7 + h, wref(h).at[:, :, core])

    def w_stage(h, number):
        for kind, route in enumerate(w_routes[h]):
            route.stage(number, lambda db, kind=kind: hand_column(me.core, kind, db).start())

    def late_stage(number):
        for route in late_routes:
            route.stage(number)

    kv_routes = [
        [
            Gather(
                me,
                kind,
                lambda z, y, h=h, kind=kind: kvbuf.at[h, kind, z, y],
                lambda ref, n: ref.at[:, n],
                kv_send.at[h, kind],
                kv_recv.at[h, kind],
            )
            for kind in range(2)
        ]
        for h in range(HEADS)
    ]

    def kv_stage(h, number):
        for route in kv_routes[h]:
            route.stage(number)

    rs_routes = [
        [
            Scatter(
                me,
                kind,
                lambda z, y, h=h, kind=kind: grads.at[h, kind, z, y],
                lambda ref, n: ref.at[:, n],
                lambda n, h=h, kind=kind: kv_halves.at[h, kind, n],
                lambda n, h=h, kind=kind: (
                    kv_columns.at[h, kind, n] if n < 2 else kv_third.at[kind]
                ),
                lambda n, h=h, kind=kind: kv_blocks.at[h, kind, n],
                rs_send.at[h, kind],
                rs_recv.at[h, kind],
            )
            for kind in range(2)
        ]
        for h in range(HEADS)
    ]

    first_span = spans_ref[0, me.rank, 0]
    second_span = spans_ref[0, me.rank, 1]
    flip = first_span > second_span
    low_span = jnp.minimum(first_span, second_span)
    high_span = jnp.maximum(first_span, second_span)

    def rs_stage(h, number):
        for kind, route in enumerate(rs_routes[h]):
            route.stage(number)
            if number < 3:
                continue
            total = route.total()
            low, high = total[0], total[1]
            total = jnp.concatenate(
                [jnp.where(flip, high, low), jnp.where(flip, low, high)], axis=0
            )
            if kind == 0:
                total = total * cos_ref[...] - pltpu.roll(total, HEAD // 2, 1) * sin_ref[...]
            else:
                total = total * (1.0 / SCALE)
            dkv[h, :, kind * HEAD : (kind + 1) * HEAD] = total.astype(BF16)

    def term_rows(h):
        return pl.ds(0, BLOCK if h == HEADS - 1 else PART)

    def pair_copy(h, j):
        return pltpu.make_async_remote_copy(
            src_ref=tref(h).at[j, :, 1 - me.core, term_rows(h)],
            dst_ref=pref(h).at[j],
            send_sem=pair_send.at[h, j],
            recv_sem=pair_recv.at[h, j],
            device_id=me.partner(),
            device_id_type=MESH,
        )

    def pair_sum(h):
        def group(j, carry):
            pair_copy(h, j).wait_recv()

            add_into(tref(h).at[j, :, me.core, term_rows(h)], [pref(h).at[j]])
            return carry

        lax.fori_loop(0, 4, group, 0)

    xr_routes = [
        RingScatter(
            me,
            lambda number, h=h: tref(h).at[:, :, me.core, piece_rows(number)],
            xr_send.at[h],
            xr_recv.at[h],
            lambda n, h=h: r_land.at[h, n],
        )
        for h in range(HEADS - 1)
    ]
    xr_routes.append(
        RingScatter(
            me,
            lambda number: x_send.at[piece_rows(number)],
            xr_send.at[HEADS - 1],
            xr_recv.at[HEADS - 1],
            lambda n: l_land.at[n],
        )
    )
    ws_routes = [
        [
            Scatter(
                me,
                kind,
                lambda z, y, h=h, kind=kind: tref(h).at[
                    z, y, me.core, piece_rows(me.x), pl.ds(kind * HEAD, HEAD)
                ],
                lambda ref, n: ref.at[:, pl.ds(16 * n, 16)],
                lambda n, h=h, kind=kind: q_halves.at[h, kind, n],
                lambda n, h=h, kind=kind: q_columns.at[h, kind, n],
                lambda n, h=h, kind=kind: q_blocks.at[h, kind, n],
                ws_send.at[h, kind],
                ws_recv.at[h, kind],
            )
            for kind in range(2)
        ]
        for h in range(HEADS - 1)
    ]
    ws_routes.append(
        [
            Scatter(
                me,
                kind,
                lambda z, y, kind=kind: t_last.at[z, y, me.core, tall_rows(kind, True)],
                lambda ref, n, kind=kind: tall_half(ref, kind, True, n),
                lambda n, kind=kind: w_halves.at[kind, n, :, pl.ds(0, 48 if kind and n else 32)],
                lambda n, kind=kind: (w_columns.at[kind, n] if n < 2 else w_third.at[kind]).at[
                    :, pl.ds(0, 80 if kind else 64)
                ],
                lambda n, kind=kind: w_blocks.at[kind, n, pl.ds(0, 80 if kind else 64)],
                ws_send.at[HEADS - 1, kind],
                ws_recv.at[HEADS - 1, kind],
            )
            for kind in range(2)
        ]
    )

    def xr_stage(h, number):
        xr_routes[h].stage(number)

    def ws_stage(h, number):
        for kind, route in enumerate(ws_routes[h]):
            route.stage(number)
            if number < 3:
                continue
            total = route.total().astype(BF16)
            if h < HEADS - 1:
                final[
                    me.core, h, piece_rows(me.x), kind * HEAD : (kind + 1) * HEAD
                ] = total
            else:
                x_send[64 * kind : 64 * kind + (80 if kind else 64), :] = total

    def columns_of(j):
        return pl.ds(pl.multiple_of(((j % 2) * 2 + j // 2) * FOUR, FOUR), FOUR)

    def unit_piece(j):
        return x_ref[:, columns_of(j)].astype(F32) * inv_ref[...]

    def weight_block(h, j):
        return wref(h)[j, :, :, 0:PART, :].reshape(FOUR, 2 * HEAD)

    def positions():
        row = lax.broadcasted_iota(jnp.int32, (ROWS, 1), 0)
        place = jnp.where(row < SPAN, first_span * SPAN + row, second_span * SPAN + row - SPAN)
        angle = place.astype(F32) * frequency_ref[...]
        lane = lax.broadcasted_iota(jnp.int32, (ROWS, HEAD), 1)
        sine = jnp.sin(angle)
        cos_ref[...] = jnp.cos(angle)
        sin_ref[...] = jnp.where(lane < HEAD // 2, -sine, sine)
        lane = lax.broadcasted_iota(jnp.int32, (1, HEAD), 1)
        for s in range(0, RANKS, 2):
            ranks = [rank_at((s + n) % 4, (s + n) // 4) for n in range(2)]
            pairs = [(spans_ref[0, r, 0], spans_ref[0, r, 1]) for r in ranks]
            for half, pick in ((0, jnp.minimum), (1, jnp.maximum)):
                left, right = pick(*pairs[0]), pick(*pairs[1])
                kpos_ref[half : half + 1, s * SPAN : s * SPAN + HEAD] = jnp.where(
                    lane < SPAN, left * SPAN + lane, right * SPAN + lane - SPAN
                )

    def normalise():
        squares = jnp.zeros((ROWS, HEAD), F32)
        for c in range(FEATURES // HEAD):
            piece = x_ref[:, c * HEAD : (c + 1) * HEAD].astype(F32)
            squares = squares + piece * piece
        inv_ref[...] = lax.rsqrt(
            jnp.sum(squares, axis=-1, keepdims=True) * (1.0 / FEATURES) + EPSILON
        )

    def prepare():
        for j in range(4):
            for y in range(4):
                gain_row[j, :, y * SHARE : (y + 1) * SHARE] = w_first[
                    j, y, 0, PART:BLOCK, :
                ].astype(F32)[0:1, :]
            normed[j] = (unit_piece(j) * gain_row[j]).astype(BF16)

    def turn():
        for j in range(4):
            normed_t[j] = jnp.transpose(normed[j].astype(F32)).astype(BF16)

    def project(h):
        raw = dot(normed[0], weight_block(h, 0))
        for j in range(1, 4):
            raw = raw + dot(normed[j], weight_block(h, j))
        key = raw[:, 0:HEAD]
        key = key * cos_ref[...] + pltpu.roll(key, HEAD // 2, 1) * sin_ref[...]
        for kind, array in ((0, key), (1, raw[:, HEAD:])):
            kvbuf[h, kind, me.z, me.y, 0] = jnp.where(flip, array[SPAN:], array[:SPAN]).astype(BF16)
            kvbuf[h, kind, me.z, me.y, 1] = jnp.where(flip, array[:SPAN], array[SPAN:]).astype(BF16)

    def weight_terms(h):
        last = h == HEADS - 1

        def group(j, mean):
            grad = dkv[h]
            back = dot_nt(grad, weight_block(h, j))
            block = dot(normed_t[j], grad).astype(BF16)
            tref(h)[j, :, :, 0:PART, :] = block.reshape(4, 2, PART, 2 * HEAD)
            if h:
                back = back + ngrad[j]
            if last:
                unit = unit_piece(j)
                gain = jnp.sum(unit * back, axis=0, keepdims=True)
                for y in range(4):
                    piece = jnp.broadcast_to(gain[:, y * SHARE : (y + 1) * SHARE], (16, SHARE))
                    for part in range(2):
                        t_last[j, y, part, PART:BLOCK, :] = piece.astype(BF16)
                back = back * gain_row[j]
                mean = mean + jnp.sum(back * unit, axis=-1, keepdims=True)
            ngrad[j] = back
            pair_copy(h, j).start()
            return mean

        return lax.fori_loop(0, 4, group, jnp.zeros((ROWS, 1), F32))

    token = lax.broadcasted_iota(jnp.int32, (WIDTH, 1), 0) % SPAN
    q_pos = (low_span * SPAN + token, high_span * SPAN + token)

    def load_head(h):
        for n in range(GROUP):
            column = pl.ds(pl.multiple_of((h * GROUP + n) * HEAD, HEAD), HEAD)
            for source, target in ((q_ref, qs), (g_ref, gs)):
                first, second = source[0:SPAN, column], source[SPAN:ROWS, column]
                target[0, n * SPAN : (n + 1) * SPAN, :] = jnp.where(flip, second, first)
                target[1, n * SPAN : (n + 1) * SPAN, :] = jnp.where(flip, first, second)

    def store_head(h):
        for n in range(GROUP):
            column = pl.ds(pl.multiple_of((h * GROUP + n) * HEAD, HEAD), HEAD)
            for source, target in ((qs, q_ref), (gs, g_ref)):
                low = source[0, n * SPAN : (n + 1) * SPAN, :]
                high = source[1, n * SPAN : (n + 1) * SPAN, :]
                target[0:SPAN, column] = jnp.where(flip, high, low)
                target[SPAN:ROWS, column] = jnp.where(flip, low, high)

    def attend(h, half):
        def block(kind, side):
            return kvbuf[h, kind, :, :, side].reshape(RANKS * SPAN, HEAD)

        place_rows = slice(half * WIDTH, (half + 1) * WIDTH)
        q, g = qs[half], gs[half]
        scores = [dot_nt(q, block(0, k)) for k in range(half + 1)]
        scores[half] = jnp.where(
            kpos_ref[half : half + 1, :] <= q_pos[half], scores[half], NEG_FILL
        )
        top = jnp.max(scores[0], axis=-1, keepdims=True)
        if half:
            top = jnp.maximum(top, jnp.max(scores[1], axis=-1, keepdims=True))
        weights = [jnp.exp2((s - top) * EXP_SCALE) for s in scores]
        total = jnp.sum(weights[0], axis=-1, keepdims=True)
        if half:
            total = total + jnp.sum(weights[1], axis=-1, keepdims=True)
        low = [w.astype(BF16) for w in weights]
        attended = dot(low[0], block(1, 0))
        if half:
            attended = attended + dot(low[1], block(1, 1))
        share = 1.0 / total
        attended = (attended * share).astype(BF16)
        grad = (g.astype(F32) * (share * SCALE)).astype(BF16)
        grad_f = grad.astype(F32)
        row_dot = jnp.sum(grad_f * attended.astype(F32), axis=-1, keepdims=True)
        gt[:, place_rows] = jnp.transpose(grad_f).astype(BF16)
        qt[:, place_rows] = jnp.transpose(q.astype(F32)).astype(BF16)
        back = None
        for k in range(half + 1):
            dots = dot_nt(grad, block(1, k))
            ds = (low[k].astype(F32) * (dots - row_dot)).astype(BF16)
            if k:
                probs_high[...] = low[k]
                ds_high[...] = ds
            else:
                probs_low[place_rows, :] = low[k]
                ds_low[place_rows, :] = ds
            term = dot(ds, block(0, k))
            back = term if back is None else back + term
        qs[half] = back.astype(BF16)
        gs[half] = attended

    def key_terms(h):
        for kind, left, low, high in ((0, qt, ds_low, ds_high), (1, gt, probs_low, probs_high)):
            for side, array in (
                (0, dot(left[...], low[...])),
                (1, dot(left[:, WIDTH:], high[...])),
            ):
                grads[h, kind, :, :, side] = (
                    jnp.transpose(array).astype(BF16).reshape(4, 4, SPAN, HEAD)
                )

    def late_arrival(h):
        wx[h].stage(1)
        hand_head(me.core, h).start()

    def late_projection(h):
        hand_head(1 - me.core, h).wait_recv()
        project(h)
        kv_stage(h, 0)

    for routes in (w_routes[0], late_routes, kv_routes[0], rs_routes[3], ws_routes[3]):
        for route in routes:
            route.direct = True
    late_stage(0)
    w_stage(0, 0)
    positions()
    loads[0].wait()
    normalise()
    late_stage(1)
    w_stage(0, 1)
    late_stage(2)
    for h in range(EARLY, HEADS):
        wx[h].stage(0)
    w_stage(0, 2)
    for kind in range(2):
        for db in range(4):
            hand_column(1 - me.core, kind, db).wait_recv()
    prepare()
    project(0)
    kv_stage(0, 0)
    turn()
    kv_stage(0, 1)
    late_arrival(1)
    loads[1].wait()
    loads[2].wait()
    load_head(0)
    late_projection(1)
    kv_stage(0, 2)

    def xr_begin(h):
        pair_sum(h)
        xr_stage(h, 0)

    def xr_end(h):
        xr_stage(h, 1)
        ws_stage(h, 0)

    def weights_left():
        for routes in w_routes + [late_routes]:
            for route in routes:
                route.drain()
        for route in wx.values():
            route.drain()
        for kind in range(2):
            for db in range(4):
                hand_column(me.core, kind, db).wait_send()
        for h in range(1, HEADS):
            hand_head(me.core, h).wait_send()

    plan = {
        (0, 0): [lambda: kv_stage(1, 1), lambda: late_arrival(2)],
        (0, 1): [lambda: late_projection(2)],
        (0, 2): [lambda: kv_stage(1, 2), lambda: kv_stage(2, 1), lambda: late_arrival(3)],
        (0, 3): [lambda: rs_stage(0, 0)],
        (0, 4): [lambda: late_projection(3), lambda: kv_stage(1, 3)],
        (1, 1): [lambda: kv_stage(2, 2), lambda: rs_stage(0, 1)],
        (1, 2): [lambda: kv_stage(3, 1), lambda: rs_stage(0, 2)],
        (1, 3): [lambda: rs_stage(1, 0)],
        (1, 4): [weights_left, lambda: kv_stage(2, 3), lambda: kv_stage(3, 2)],
        (2, 1): [lambda: rs_stage(0, 3), lambda: weight_terms(0), lambda: rs_stage(1, 1)],
        (2, 2): [lambda: xr_begin(0), lambda: rs_stage(1, 2)],
        (2, 3): [lambda: rs_stage(2, 0)],
        (2, 4): [lambda: rs_stage(1, 3), lambda: weight_terms(1), lambda: kv_stage(3, 3)],
        (3, 1): [lambda: rs_stage(2, 1), lambda: xr_begin(1)],
        (3, 2): [lambda: rs_stage(2, 2), lambda: xr_end(0)],
        (3, 3): [lambda: rs_stage(3, 0), lambda: ws_stage(0, 1)],
        (3, 4): [lambda: rs_stage(2, 3), lambda: weight_terms(2)],
    }

    def one_head(h, carry):
        def serve(point):
            for head in range(HEADS):
                if (head, point) not in plan:
                    continue

                @pl.when(h == head)
                def _():
                    for item in plan[head, point]:
                        item()

        serve(0)
        attend(h, 0)
        serve(1)
        attend(h, 1)
        serve(2)
        key_terms(h)
        serve(3)
        store_head(h)

        @pl.when(h < HEADS - 1)
        def _():
            load_head(h + 1)

        serve(4)
        return carry

    lax.fori_loop(0, HEADS, one_head, 0)

    stores = [
        pltpu.make_async_copy(g_ref, out_hbm, io_sem.at[0]),
        pltpu.make_async_copy(q_ref, dq_hbm, io_sem.at[1]),
    ]
    for copy in stores:
        copy.start()

    def x_copy(index, ref, dst, to):
        return pltpu.make_async_remote_copy(
            src_ref=ref,
            dst_ref=dst,
            send_sem=x_ssem.at[index],
            recv_sem=x_rsem.at[index],
            device_id=to,
            device_id_type=MESH,
        )

    def spread(base, heads, d, owner):
        ref = final.at[me.core, heads, piece_rows(owner)]
        return x_copy(base + d - 1, ref, ref, me.along_x(d))

    def to_partner(index, heads, core):
        ref = final.at[core, heads]
        return x_copy(index, ref, ref, me.partner())

    def spread_start(base, heads):
        for d in (1, 2, 3):
            spread(base, heads, d, me.x).start()

    def spread_wait(base, heads):
        for d in (1, 2, 3):
            spread(base, heads, d, (me.x + 4 - d) % 4).wait_recv()

    early_heads, late_head = pl.ds(0, HEADS - 1), pl.ds(HEADS - 1, 1)
    xr_begin(2)
    ws_stage(0, 2)
    rs_stage(3, 2)
    xr_end(1)
    ws_stage(0, 3)
    rs_stage(3, 3)
    mean = weight_terms(3) * (1.0 / FEATURES)
    pair_sum(3)
    ws_stage(3, 0)
    ws_stage(1, 1)

    def row_grad(j, carry):
        dx = inv_ref[...] * (ngrad[j] - unit_piece(j) * mean)
        x_ref[:, columns_of(j)] = dx.astype(BF16)
        return carry

    lax.fori_loop(0, 4, row_grad, 0)
    stores.append(pltpu.make_async_copy(x_ref, dx_hbm, io_sem.at[2]))
    stores[2].start()
    ws_stage(1, 2)
    xr_end(2)
    ws_stage(3, 2)
    ws_stage(1, 3)
    ws_stage(2, 1)
    ws_stage(3, 3)
    xr_stage(3, 0)
    gains = [
        x_copy(5 + d, x_send.at[pl.ds(PART, 16)], x_gain.at[d - 1], me.along_x(d))
        for d in (1, 2, 3)
    ]
    for copy in gains:
        copy.start()
    ws_stage(2, 2)
    xr_stage(3, 1)
    final[me.core, HEADS - 1, piece_rows(me.x)] = x_send[piece_rows(me.x), :]
    spread_start(3, late_head)
    ws_stage(2, 3)
    spread_start(0, early_heads)
    spread_wait(0, early_heads)
    to_partner(9, early_heads, me.core).start()
    for copy in gains:
        copy.wait_recv()
    total = x_send[PART:BLOCK, :].astype(F32)
    for d in range(3):
        total = total + x_gain[d].astype(F32)
    dgain_ref[...] = total[0:8, :]
    spread_wait(3, late_head)
    to_partner(10, late_head, me.core).start()

    def write_weights(heads):
        for h in heads:
            for core in range(2):
                rows, columns = slice(core * PART, (core + 1) * PART), slice(h * HEAD, (h + 1) * HEAD)
                dwk_ref[rows, columns] = final[core, h, :, 0:HEAD].astype(F32)
                dwv_ref[rows, columns] = final[core, h, :, HEAD:].astype(F32)

    to_partner(9, early_heads, 1 - me.core).wait_recv()
    write_weights(range(HEADS - 1))
    to_partner(10, late_head, 1 - me.core).wait_recv()
    write_weights((HEADS - 1,))

    for routes in kv_routes + rs_routes + ws_routes:
        for route in routes:
            route.drain()
    for route in xr_routes:
        route.drain()
    for h in range(HEADS):
        for j in range(4):
            pair_copy(h, j).wait_send()
    for copy in gains:
        copy.wait_send()
    for base, heads in ((0, early_heads), (3, late_head)):
        for d in (1, 2, 3):
            spread(base, heads, d, me.x).wait_send()
    to_partner(9, early_heads, me.core).wait_send()
    to_partner(10, late_head, me.core).wait_send()
    for copy in stores:
        copy.wait()


def settle(*refs):
    for n in range(5):
        refs[6 + n][...] = refs[n][...]
    refs[11][...] = refs[5][0, :]


def local(inputs, queries, out_grad, span_ids, norm_gain, key_weight, value_weight):
    frequency = np.exp(
        -math.log(ROPE_BASE) * (2.0 * np.arange(HEAD // 2, dtype=np.float32) / HEAD)
    ).astype(np.float32)
    frequency = jnp.asarray(np.concatenate([frequency, frequency])[None, :])
    anywhere = pl.BlockSpec(memory_space=pl.ANY)
    vmem = pl.BlockSpec(memory_space=pltpu.VMEM)
    smem = pl.BlockSpec(memory_space=pltpu.SMEM)
    dma = pltpu.SemaphoreType.DMA
    outs = pl.pallas_call(
        kernel,
        out_shape=[
            jax.ShapeDtypeStruct((ROWS, FEATURES), BF16),
            jax.ShapeDtypeStruct((ROWS, FEATURES), BF16),
            jax.ShapeDtypeStruct((ROWS, FEATURES), BF16),
            jax.ShapeDtypeStruct((SHARE, WIDTH), F32),
            jax.ShapeDtypeStruct((SHARE, WIDTH), F32),
            jax.ShapeDtypeStruct((8, SHARE), F32),
        ],
        in_specs=[anywhere] * 3 + [smem, vmem] + [anywhere] * 2 + [vmem],
        out_specs=[anywhere] * 3 + [vmem] * 3,
        scratch_shapes=[
            pltpu.VMEM((ROWS, FEATURES), BF16),
            pltpu.VMEM((ROWS, FEATURES), BF16),
            pltpu.VMEM((ROWS, FEATURES), BF16),
            pltpu.VMEM((4, 4, 2, BLOCK, 2 * HEAD), BF16),
            pltpu.VMEM((HEADS - 1, 4, 4, 2, PART, 2 * HEAD), BF16),
            pltpu.VMEM((HEADS, 2, 4, 4, 2, SPAN, HEAD), BF16),
            pltpu.VMEM((2, WIDTH, HEAD), BF16),
            pltpu.VMEM((2, WIDTH, HEAD), BF16),
            pltpu.VMEM((HEAD, 2 * WIDTH), BF16),
            pltpu.VMEM((HEAD, 2 * WIDTH), BF16),
            pltpu.VMEM((2 * WIDTH, RANKS * SPAN), BF16),
            pltpu.VMEM((WIDTH, RANKS * SPAN), BF16),
            pltpu.VMEM((2 * WIDTH, RANKS * SPAN), BF16),
            pltpu.VMEM((WIDTH, RANKS * SPAN), BF16),
            pltpu.VMEM((HEADS, 2, 4, 4, 2, SPAN, HEAD), BF16),
            pltpu.VMEM((HEADS, 2, 2, 4, SPAN, HEAD), BF16),
            pltpu.VMEM((HEADS, 2, 2, 4, 2, SPAN, HEAD), BF16),
            pltpu.VMEM((2, 4, 2, SPAN, HEAD), BF16),
            pltpu.VMEM((HEADS, 2, 3, 2, SPAN, HEAD), BF16),
            pltpu.VMEM((HEADS, ROWS, 2 * HEAD), BF16),
            pltpu.VMEM((4, ROWS, FOUR), F32),
            pltpu.VMEM((4, ROWS, FOUR), BF16),
            pltpu.VMEM((4, FOUR, ROWS), BF16),
            pltpu.VMEM((4, 1, FOUR), F32),
            pltpu.VMEM((4, 4, 2, BLOCK, 2 * HEAD), BF16),
            pltpu.VMEM((4, 4, BLOCK, 2 * HEAD), BF16),
            pltpu.VMEM((HEADS - 1, 4, 4, PART, 2 * HEAD), BF16),
            pltpu.VMEM((HEADS - 1, 2, 2, 4, 16, HEAD), BF16),
            pltpu.VMEM((HEADS - 1, 2, 2, 4, 32, HEAD), BF16),
            pltpu.VMEM((HEADS - 1, 2, 3, 32, HEAD), BF16),
            pltpu.VMEM((2, 2, 4, 48, 2 * HEAD), BF16),
            pltpu.VMEM((2, 2, 4, 80, 2 * HEAD), BF16),
            pltpu.VMEM((2, 4, 80, 2 * HEAD), BF16),
            pltpu.VMEM((2, 3, 80, 2 * HEAD), BF16),
            pltpu.VMEM((HEADS - 1, 3, 4, 4, 32, 2 * HEAD), BF16),
            pltpu.VMEM((3, 32, 2 * HEAD), BF16),
            pltpu.VMEM((BLOCK, 2 * HEAD), BF16),
            pltpu.VMEM((3, 16, 2 * HEAD), BF16),
            pltpu.VMEM((2, HEADS, PART, 2 * HEAD), BF16),
            pltpu.VMEM((ROWS, 1), F32),
            pltpu.VMEM((2, RANKS * SPAN), jnp.int32),
            pltpu.VMEM((ROWS, HEAD), F32),
            pltpu.VMEM((ROWS, HEAD), F32),
            dma((3 + 2 * HEADS,)),
            dma((EARLY + 1, 2, 7)), dma((EARLY + 1, 2, 7)),
            dma((7 + HEADS,)), dma((7 + HEADS,)),
            dma((HEADS - EARLY, 3)), dma((HEADS - EARLY, 3)),
            dma((HEADS, 2, 7)), dma((HEADS, 2, 7)),
            dma((HEADS, 2, 7)), dma((HEADS, 2, 7)),
            dma((HEADS, 4)), dma((HEADS, 4)),
            dma((HEADS, 2, 7)), dma((HEADS, 2, 7)),
            dma((HEADS, 3)), dma((HEADS, 3)),
            dma((11,)), dma((11,)),
        ],
        compiler_params=pltpu.CompilerParams(
            collective_id=0, has_side_effects=True, vmem_limit_bytes=55 * 1024 * 1024
        ),
        cost_estimate=pl.CostEstimate(
            flops=12 * 10**9, bytes_accessed=10**7, transcendentals=7 * 10**6
        ),
        name="layer",
    )(
        inputs, queries, out_grad, span_ids, norm_gain, key_weight, value_weight, frequency
    )
    blocks = [pl.BlockSpec((ROWS, FEATURES // 4), lambda i: (0, i))] * 3
    blocks += [pl.BlockSpec((SHARE // 4, WIDTH), lambda i: (i, 0))] * 2
    gains = [pl.BlockSpec((8, SHARE), lambda i: (0, 0)), pl.BlockSpec((SHARE,), lambda i: (0,))]
    outs = pl.pallas_call(
        settle,
        out_shape=[jax.ShapeDtypeStruct(o.shape, o.dtype) for o in outs[:5]]
        + [jax.ShapeDtypeStruct((SHARE,), F32)],
        grid=(4,),
        in_specs=blocks + gains[:1],
        out_specs=blocks + gains[1:],
        name="settle",
    )(*outs)
    return tuple(outs)


def solution(mesh):
    tokens = P(("dp", "shard", "ctx"), None)
    rows = P(("shard", "ctx"), None)
    return jax.shard_map(
        local,
        mesh=mesh,
        in_specs=(tokens, tokens, tokens, P("dp", None, None), P(("shard", "ctx")), rows, rows),
        out_specs=(tokens, tokens, tokens, rows, rows, P(("shard", "ctx"))),
        check_vma=False,
    )
```
